32 devices in a mesh: row: 8 (over z, y), col: 4 (over x, core).
Axes of the slice: x: 2, y: 2, z: 4, core: 2. Of those that a mesh axis runs over, the one named last changes fastest.
Arguments:
- start_vectors: float32 [64, 4096], P(None, ('row', 'col')), may hold values from -6 to 6
- cluster_order: int32 [32, 128], P(('row', 'col')), may hold values from 0 to 127, each once within a row
- weights: bfloat16 [4096, 4, 1024], P('row', 'col'), may hold values from 0 to 1, as said below
- block_mask: int32 [32, 4, 8], P('row', 'col'), may hold values 0 or 1
Outputs:
- embedding: float32 [64, 4096], P(None, ('row', 'col'))
The draws below stay inside these ranges and needn't reach their ends.
Inputs may be any that keep to these rules, and one draw needn't show every extreme that they name: Each row of cluster_order holds every number of 0 to 127 once. `block_mask`: entries below the diagonal blocks are read only through their mirror. `weights`: every node except the last of its cluster block has a positive weight to the next node of its cluster block.
All inputs are finite; a program needn't handle non-finite values.
Results may differ from the reference program's by a relative error of at most 0.00087.
Values may be sent and summed in bfloat16 or wider, within the bound.
No kernel may reach another device: no remote copies, remote signals or barrier semaphores. Data moves between devices by JAX's collectives and lax.ppermute only.
A program may use at most 64 MiB of HBM per device.

```python
import jax
import jax.numpy as jnp
from jax import lax

K = 64
NODE_DEV = 128
ITERS = 3
BLOCKS = 32
NODES = 4096
N_ROW = 8
N_COL = 4


def draw_weights(key, part):
    width = N_ROW * NODE_DEV
    near_share = min(1.0, 16.0 / NODE_DEV)
    far_share = min(1.0, 72.0 / (NODE_DEV * BLOCKS))
    entry = jnp.arange(width, dtype=jnp.int32)
    col_j = jnp.arange(N_COL, dtype=jnp.int32)
    col_nodes = ((entry // NODE_DEV)[None, :] * N_COL + col_j[:, None]) * NODE_DEV + (entry % NODE_DEV)[None, :]

    def one_block(block_id):
        block_key = jax.random.fold_in(key, block_id)
        keep_key, value_key = jax.random.split(block_key)
        row_nodes = block_id * NODE_DEV + jnp.arange(NODE_DEV, dtype=jnp.int32)
        same_block = (col_nodes // NODE_DEV)[None, :, :] == block_id
        chain_link = same_block & (col_nodes[None, :, :] == row_nodes[:, None, None] + 1)
        share = jnp.where(same_block, jnp.float32(near_share), jnp.float32(far_share))
        roll = jax.random.uniform(keep_key, (NODE_DEV, N_COL, width), jnp.float32)
        linked = (roll < share) | chain_link
        fresh = jax.random.uniform(value_key, (NODE_DEV, N_COL, width), jnp.float32)
        values = 0.05 + 0.95 * fresh
        return jnp.where(linked, values, jnp.float32(0.0)).astype(jnp.bfloat16)
    stacked = lax.map(one_block, jnp.arange(BLOCKS, dtype=jnp.int32))
    return stacked.reshape(NODES, N_COL, width)


def place_ends(entries, key, low, largest):
    longest = entries.shape.index(max(entries.shape))
    spots = []
    for shift in (0, 1):
        where = [jax.random.randint(jax.random.fold_in(key, axis), (), 0, length) for axis, length in enumerate(entries.shape)]
        where[longest] = (where[longest] + shift) % entries.shape[longest]
        spots.append(tuple(where))
    return entries.at[spots[0]].set(low).at[spots[1]].set(largest)


def block_levels(rng, shape, cuts, low, largest):
    factor_of, own = 1.0, jax.random.fold_in(rng, 6)
    for axis_at, blocks in cuts:
        steps = jnp.exp(jax.random.uniform(jax.random.fold_in(own, axis_at), (blocks,), jnp.float32, low / len(cuts), largest / len(cuts)))
        factor_of = factor_of * jnp.repeat(steps, shape[axis_at] // blocks).reshape([-1 if axis == axis_at else 1 for axis in range(len(shape))])
    return factor_of


def gaussian(own_key, dims, spread, reach, cuts=(), kind=jnp.bfloat16):
    level = block_levels(own_key, dims, cuts, -0.22, 0.18) if cuts else 1.0
    drawn = jax.random.normal(own_key, dims, jnp.float32) * spread * level
    return jnp.minimum(jnp.maximum(drawn, -reach), reach).astype(kind)


def setup_inputs(seed: int = 0) -> dict:
    keys = jax.random.split(jax.random.key(seed), 5)
    return {
        "start_vectors": gaussian(keys[0], (K, NODES), 1.0, 6.0, ((1, 32),), jnp.float32),
        "cluster_order": jax.vmap(lambda own: jax.random.permutation(own, NODE_DEV))(jax.random.split(keys[1], BLOCKS)).reshape((BLOCKS, NODE_DEV)).astype(jnp.int32),
        "weights": draw_weights(jax.random.fold_in(keys[4], 71), 0),
        "block_mask": place_ends((jax.random.randint(keys[3], (BLOCKS, N_COL, N_ROW), 0, 3) < 1).astype(jnp.int32), jax.random.fold_in(keys[3], 1), 0, 1),
    }


def orthonormalize(panel_in):
    gram_matrix = jnp.dot(panel_in.astype(jnp.float32), panel_in.T.astype(jnp.float32), precision=lax.Precision.HIGHEST, preferred_element_type=jnp.float32)
    factor = jnp.linalg.cholesky(gram_matrix)
    return jax.scipy.linalg.solve_triangular(factor, panel_in, lower=True)

def block_row(weights, block_mask, block_id):
    stored = lax.dynamic_slice_in_dim(weights, block_id * NODE_DEV, NODE_DEV, 0)
    stored = stored.reshape(NODE_DEV, N_COL, N_ROW, NODE_DEV).transpose(0, 2, 1, 3).reshape(NODE_DEV, NODES)
    mask_row = lax.dynamic_index_in_dim(block_mask, block_id, 0, keepdims=False).T.reshape(BLOCKS)
    span_ids = jnp.arange(BLOCKS, dtype=jnp.int32)
    live_cols = jnp.repeat((mask_row > 0) | (span_ids == block_id), NODE_DEV)
    row_nodes = block_id * NODE_DEV + jnp.arange(NODE_DEV, dtype=jnp.int32)
    col_nodes = jnp.arange(NODES, dtype=jnp.int32)
    keep_upper = live_cols[None, :] & (row_nodes[:, None] < col_nodes[None, :])
    return jnp.where(keep_upper, stored, jnp.zeros((), stored.dtype))

def apply_graph(weights, block_mask, vectors):

    def visit(carry, block_id):
        upper_rows = block_row(weights, block_mask, block_id)
        direct = jnp.dot(vectors.astype(jnp.float32), upper_rows.T.astype(jnp.float32), preferred_element_type=jnp.float32)
        local_vec = lax.dynamic_slice_in_dim(vectors, block_id * NODE_DEV, NODE_DEV, 1)
        carry = carry + jnp.dot(local_vec.astype(jnp.float32), upper_rows.astype(jnp.float32), preferred_element_type=jnp.float32)
        return (carry, direct)
    initial_sum = jnp.zeros((vectors.shape[0], NODES), jnp.float32)
    mirrored, direct_rows = lax.scan(visit, initial_sum, jnp.arange(BLOCKS, dtype=jnp.int32))
    direct_all = direct_rows.transpose(1, 0, 2).reshape(vectors.shape[0], NODES)
    return direct_all + mirrored

def reference(start_vectors, cluster_order, weights, block_mask):
    ones_row = jnp.ones((1, NODES), weights.dtype)
    degree = apply_graph(weights, block_mask, ones_row)
    inverse_root = 1.0 / jnp.sqrt(degree)
    reshaped = start_vectors.reshape(K, BLOCKS, NODE_DEV)
    picked = jnp.take_along_axis(reshaped, jnp.broadcast_to(cluster_order[None], reshaped.shape), axis=2)
    panel_now = orthonormalize(picked.reshape(K, NODES))
    for round_index in range(ITERS):
        vectors = (inverse_root * panel_now).astype(jnp.bfloat16)
        product = apply_graph(weights, block_mask, vectors)
        panel_now = orthonormalize(panel_now + inverse_root * product)
    return jnp.sqrt(jnp.float32(NODES)) * panel_now
```

```python
import math

import jax
import jax.numpy as jnp
from jax import lax
from jax.experimental import pallas as pl
from jax.experimental.pallas import tpu as pltpu
from jax.sharding import PartitionSpec as P

ITERS = 3
HIGHEST = lax.Precision.HIGHEST
F32 = jnp.float32
BF16 = jnp.bfloat16


def dot(a, b, contract, precision=None):
    return lax.dot_general(
        a, b, ((contract[0], contract[1]), ((), ())), precision=precision, preferred_element_type=F32
    )


def lanes(blocks):
    return jnp.concatenate(blocks, axis=1)


def inverse_factor(gram):
    k = gram.shape[0]
    rows = lax.broadcasted_iota(jnp.int32, (k, 1), 0)
    diagonal = rows == lax.broadcasted_iota(jnp.int32, (k, k), 1)
    work = lanes([gram, diagonal.astype(F32)])
    for step in range(k):
        ratio = work[:, step : step + 1] / work[step : step + 1, step : step + 1]
        work = work - jnp.where(rows > step, ratio, 0.0) * work[step : step + 1, :]
    pivots = jnp.sum(jnp.where(diagonal, work[:, :k], 0.0), axis=1, keepdims=True)
    return work[:, k:] * (1.0 / jnp.sqrt(pivots))


def prepare_kernel(width, mask_ref, stored_ref, start_ref, order_ref, by_row_ref, by_col_ref, piece_ref):
    cols, rows = mask_ref.shape
    here_row, here_col = lax.axis_index("row"), lax.axis_index("col")
    upper = (
        lax.broadcasted_iota(jnp.int32, (width, width), 0) < lax.broadcasted_iota(jnp.int32, (width, width), 1)
    ).astype(F32)
    for j in range(cols):
        row_block = here_row * cols + j
        for i in range(rows):
            col_block = i * cols + here_col
            whole = jnp.where((mask_ref[j, i] > 0) & (row_block < col_block), 1.0, 0.0)
            partly = jnp.where(row_block == col_block, 1.0, 0.0)
            keep = (whole + partly * upper).astype(BF16)
            block = stored_ref[j * width : (j + 1) * width, i * width : (i + 1) * width] * keep
            by_row_ref[j, :, i * width : (i + 1) * width] = block
            by_col_ref[i, j * width : (j + 1) * width, :] = block
    slots = lax.broadcasted_iota(jnp.int32, (width, width), 0)
    chosen = (slots == order_ref[...]).astype(F32)
    picked = dot(start_ref[...], chosen, ((1,), (0,)), HIGHEST)
    k = picked.shape[0]
    degrees = [
        dot(jnp.ones((8, cols * width), BF16), by_col_ref[i], ((1,), (0,)))[0:1] for i in range(rows)
    ] + [dot(jnp.ones((8, rows * width), BF16), by_row_ref[j], ((1,), (1,)))[0:1] for j in range(cols)]
    spare = piece_ref.shape[1] - k - rows - cols
    if spare:
        degrees.append(jnp.zeros((spare, width), F32))
    degrees = jnp.concatenate(degrees, axis=0)
    for i in range(rows):
        piece_ref[i, :k] = picked
        piece_ref[i, k:] = degrees


def first_kernel(k, all_ref, vectors_ref, roots_ref, own_ref):
    cols, rows, _, width = all_ref.shape
    here_row, here_col = lax.axis_index("row"), lax.axis_index("col")
    for c in range(cols):
        part = all_ref[c, 0, k : k + rows]
        for i in range(1, rows):
            part = part + all_ref[c, i, k : k + rows]
        for i in range(rows):
            other = all_ref[0, i, k + rows + c : k + rows + c + 1]
            for e in range(1, cols):
                other = other + all_ref[e, i, k + rows + c : k + rows + c + 1]
            roots_ref[c, i : i + 1] = 1.0 / jnp.sqrt(part[i : i + 1] + other)
    gram = jnp.zeros((k, k), F32)
    for c in range(cols):
        panel = lanes([all_ref[c, i, :k] for i in range(rows)])
        gram = gram + dot(panel, panel, ((1,), (1,)), HIGHEST)
    factor = inverse_factor(gram)
    for c in range(cols):
        panel = dot(factor, lanes([all_ref[c, i, :k] for i in range(rows)]), ((1,), (0,)), HIGHEST)
        for i in range(rows):
            vectors_ref[c, i] = (panel[:, i * width : (i + 1) * width] * roots_ref[c, i : i + 1]).astype(BF16)
    own_ref[...] = dot(factor, all_ref[here_col, here_row, :k], ((1,), (0,)), HIGHEST)


def product(vectors_of, by_row_ref, by_col_ref):
    cols, rows = by_row_ref.shape[0], by_col_ref.shape[0]
    total = None
    for c in range(cols):
        term = dot(lanes([vectors_of(c, i) for i in range(rows)]), by_row_ref[c], ((1,), (1,)))
        total = term if total is None else total + term
    for i in range(rows):
        total = total + dot(lanes([vectors_of(c, i) for c in range(cols)]), by_col_ref[i], ((1,), (0,)))
    return total


def own_root(roots_ref):
    here_row, here_col = lax.axis_index("row"), lax.axis_index("col")
    return roots_ref[here_col, pl.ds(here_row, 1)]


def step_one_kernel(vectors_ref, own_ref, roots_ref, by_row_ref, by_col_ref, out_ref):
    total = product(lambda c, i: vectors_ref[c, i], by_row_ref, by_col_ref)
    image = own_ref[...] + own_root(roots_ref) * total
    for i in range(out_ref.shape[0]):
        out_ref[i] = image


def raw_image(panel_ref, roots_ref, by_row_ref, by_col_ref, scratch):
    cols, rows, k, _ = panel_ref.shape
    here_row, here_col = lax.axis_index("row"), lax.axis_index("col")
    for c in range(cols):
        for i in range(rows):
            value = panel_ref[c, i] * roots_ref[c, i : i + 1]
            high = value.astype(BF16)
            scratch[c, i, :k] = high
            scratch[c, i, k:] = (value - high.astype(F32)).astype(BF16)
    total = product(lambda c, i: scratch[c, i], by_row_ref, by_col_ref)
    return panel_ref[here_col, here_row] + own_root(roots_ref) * (total[:k] + total[k:])


def step_kernel(panel_ref, roots_ref, by_row_ref, by_col_ref, out_ref, scratch):
    image = raw_image(panel_ref, roots_ref, by_row_ref, by_col_ref, scratch)
    for i in range(out_ref.shape[0]):
        out_ref[i] = image


def last_step_kernel(panel_ref, roots_ref, by_row_ref, by_col_ref, factor_ref, out_ref, gram_ref, scratch):
    image = raw_image(panel_ref, roots_ref, by_row_ref, by_col_ref, scratch)
    image = dot(factor_ref[...], image, ((1,), (0,)), HIGHEST)
    out_ref[...] = image
    gram = dot(image, image, ((1,), (1,)), HIGHEST)
    half = gram.shape[0] // 2
    gram = lanes([gram[:half], gram[half:]])
    for i in range(gram_ref.shape[0]):
        gram_ref[i] = gram


def panel_gram(panel_ref):
    cols, rows, k, _ = panel_ref.shape
    gram = jnp.zeros((k, k), F32)
    for c in range(cols):
        panel = lanes([panel_ref[c, i] for i in range(rows)])
        gram = gram + dot(panel, panel, ((1,), (1,)), HIGHEST)
    return gram


def congruent(factor, gram):
    half = dot(factor, gram, ((1,), (0,)), HIGHEST)
    return dot(half, factor, ((1,), (1,)), HIGHEST)


def factor_kernel(panel_ref, factor_ref):
    factor_ref[...] = inverse_factor(panel_gram(panel_ref))


def next_factor_kernel(panel_ref, before_ref, factor_ref):
    factor_ref[...] = inverse_factor(congruent(before_ref[...], panel_gram(panel_ref)))


def finish_kernel(scale, grams_ref, factor_ref, image_ref, out_ref):
    packed = grams_ref[0]
    for c in range(1, grams_ref.shape[0]):
        packed = packed + grams_ref[c]
    k = factor_ref.shape[0]
    gram = jnp.concatenate([packed[:, :k], packed[:, k:]], axis=0)
    factor = inverse_factor(congruent(factor_ref[...], gram))
    image = dot(factor_ref[...], image_ref[...], ((1,), (0,)), HIGHEST)
    out_ref[...] = scale * dot(factor, image, ((1,), (0,)), HIGHEST)


def kernel_call(body, outs, *operands, scratch=(), smem=0, flops=0):
    sizes = [math.prod(a.shape) * a.dtype.itemsize for a in (*operands, *outs)]
    spec = pl.BlockSpec(memory_space=pltpu.VMEM)
    held = sum(sizes) + sum(math.prod(s.shape) * 2 for s in scratch)
    single = len(outs) == 1
    return pl.pallas_call(
        body,
        out_shape=outs[0] if single else tuple(outs),
        in_specs=[pl.BlockSpec(memory_space=pltpu.SMEM)] * smem + [spec] * (len(operands) - smem),
        out_specs=spec if single else (spec,) * len(outs),
        scratch_shapes=list(scratch),
        cost_estimate=pl.CostEstimate(flops=flops, bytes_accessed=sum(sizes), transcendentals=0),
        compiler_params=pltpu.CompilerParams(vmem_limit_bytes=held + held // 4 + (8 << 20)),
    )(*operands)


def gather_all(copies):
    return lax.all_gather(lax.all_to_all(copies, "row", 0, 0, tiled=True), "col", axis=0, tiled=False)


def local(start_vectors, cluster_order, weights, block_mask):
    rows, cols = lax.axis_size("row"), lax.axis_size("col")
    k, width = start_vectors.shape
    shape = jax.ShapeDtypeStruct
    extra = -(-(rows + cols) // 8) * 8
    by_row, by_col, piece = kernel_call(
        lambda *refs: prepare_kernel(width, *refs),
        [
            shape((cols, width, rows * width), BF16),
            shape((rows, cols * width, width), BF16),
            shape((rows, k + extra, width), F32),
        ],
        block_mask[:, 0, :],
        weights[:, 0, :],
        start_vectors,
        cluster_order,
        smem=1,
    )
    by_row = lax.all_to_all(by_row, "col", 0, 0, tiled=True)
    by_col = lax.all_to_all(by_col, "row", 0, 0, tiled=True)
    vectors, roots, own = kernel_call(
        lambda *refs: first_kernel(k, *refs),
        [shape((cols, rows, k, width), BF16), shape((cols, rows, width), F32), shape((k, width), F32)],
        gather_all(piece),
    )
    copies = shape((rows, k, width), F32)
    factor_shape = shape((k, k), F32)
    split = [pltpu.VMEM((cols, rows, 2 * k, width), BF16)]
    panel = gather_all(kernel_call(step_one_kernel, [copies], vectors, own, roots, by_row, by_col))
    image = kernel_call(step_kernel, [copies], panel, roots, by_row, by_col, scratch=split)
    factor = kernel_call(factor_kernel, [factor_shape], panel)
    panel = gather_all(image)
    image, gram = kernel_call(
        last_step_kernel,
        [shape((k, width), F32), shape((rows, k // 2, 2 * k), F32)],
        panel,
        roots,
        by_row,
        by_col,
        factor,
        scratch=split,
    )
    factor = kernel_call(next_factor_kernel, [factor_shape], panel, factor)
    gram = lax.all_to_all(gram, "row", 0, 0, tiled=True).sum(axis=0)
    gram = lax.all_gather(gram, "col", axis=0, tiled=False)
    scale = math.sqrt(width * rows * cols)
    return kernel_call(
        lambda *refs: finish_kernel(scale, *refs), [shape((k, width), F32)], gram, factor, image
    )


def solution(mesh):
    placed = (
        P(None, ("row", "col")),
        P(("row", "col"), None),
        P("row", "col", None),
        P("row", "col", None),
    )
    return jax.shard_map(
        local, mesh=mesh, in_specs=placed, out_specs=P(None, ("row", "col")), check_vma=False
    )
```

```python
import math

import jax
import jax.numpy as jnp
from jax import lax
from jax.experimental import pallas as pl
from jax.experimental.pallas import tpu as pltpu
from jax.sharding import PartitionSpec as P

ITERS = 3
HIGHEST = lax.Precision.HIGHEST
F32 = jnp.float32
BF16 = jnp.bfloat16


def dot(a, b, contract, precision=None):
    return lax.dot_general(
        a, b, ((contract[0], contract[1]), ((), ())), precision=precision, preferred_element_type=F32
    )


def lanes(blocks):
    return jnp.concatenate(blocks, axis=1)


def inverse_factor(gram, tile=8):
    k = gram.shape[0]
    diagonal = lax.broadcasted_iota(jnp.int32, (k, k), 0) == lax.broadcasted_iota(jnp.int32, (k, k), 1)
    work = lanes([diagonal.astype(F32), gram])
    tiles = [work[at : at + tile] for at in range(0, k, tile)]
    row = lax.broadcasted_iota(jnp.int32, (tile, 2 * k), 0)

    def spread(part):
        return jnp.broadcast_to(part, (tile, 2 * k))

    done = []
    for b in range(len(tiles)):
        live = range(b, len(tiles))
        first = k + tile * b
        column = {
            (q, t): spread(tiles[t][:, first + q : first + q + 1]) for q in range(tile) for t in live
        }
        pivots = jnp.ones((tile, 2 * k), F32)
        for q in range(tile):
            pivot = spread(column[q, b][q : q + 1])
            pivots = jnp.where(row == q, pivot, pivots)
            inverse = 1.0 / pivot
            ratio = {t: column[q, t] * inverse for t in live}
            ratio[b] = jnp.where(row > q, ratio[b], 0.0)
            for later in range(q + 1, tile):
                entry = spread(column[later, b][q : q + 1])
                for t in live:
                    column[later, t] = column[later, t] - ratio[t] * entry
            line = spread(tiles[b][q : q + 1])
            for t in live:
                tiles[t] = tiles[t] - ratio[t] * line
        done.append((tiles[b] * (1.0 / jnp.sqrt(pivots)))[:, :k])
    return jnp.concatenate(done, axis=0)


def slots(cols):
    parity = lax.rem(lax.axis_index("col"), 2)
    return [2 * x + parity for x in range(cols // 2)] + [2 * x + 1 - parity for x in range(cols // 2)]


def slot_of(column, cols):
    other = lax.rem(column + lax.axis_index("col"), 2)
    return other * (cols // 2) + column // 2


def prepare_kernel(sizes, mask_hbm, stored_hbm, start_hbm, order_hbm, to_rows_ref, *refs):
    rows, cols, width = sizes
    to_cols, (piece_ref, picked_ref) = refs[:cols], refs[cols : cols + 2]
    mask_ref, stored_ref, start_ref, order_ref, arrived = refs[cols + 2 :]
    here_row, here_col = lax.axis_index("row"), lax.axis_index("col")
    columns = slots(cols)
    copies = [
        pltpu.make_async_copy(mask_hbm, mask_ref, arrived.at[cols]),
        pltpu.make_async_copy(start_hbm, start_ref, arrived.at[cols + 1]),
        pltpu.make_async_copy(order_hbm, order_ref, arrived.at[cols + 2]),
    ]
    lines = [
        pltpu.make_async_copy(
            stored_hbm.at[pl.ds(pl.multiple_of(columns[s] * width, width), width)], stored_ref.at[s], arrived.at[s]
        )
        for s in range(cols)
    ]
    for copy in copies + lines:
        copy.start()
    upper = (
        lax.broadcasted_iota(jnp.int32, (width, width), 0) < lax.broadcasted_iota(jnp.int32, (width, width), 1)
    ).astype(F32)
    node = lax.broadcasted_iota(jnp.int32, (width, width), 0)
    for copy in copies:
        copy.wait()
    picked = dot(start_ref[...], (node == order_ref[...]).astype(F32), ((1,), (0,)), HIGHEST)
    picked_ref[...] = picked
    ones = jnp.ones((8, rows * width), BF16)
    line_degrees = []
    for s in range(cols):
        lines[s].wait()
        row_block = here_row * cols + columns[s]
        line = []
        for i in range(rows):
            col_block = i * cols + here_col
            whole = jnp.where((mask_ref[columns[s], i] > 0) & (row_block < col_block), 1.0, 0.0)
            partly = jnp.where(row_block == col_block, 1.0, 0.0)
            keep = (whole + partly * upper).astype(BF16)
            line.append(stored_ref[s, :, i * width : (i + 1) * width] * keep)
            to_rows_ref[i, s * width : (s + 1) * width] = line[i]
        line_degrees.append(dot(ones, lanes(line), ((1,), (1,)))[0:1])
    for distance in range(cols):
        s = slot_of(lax.rem(here_col + distance, cols), cols)
        from_line = pl.ds(pl.multiple_of(s * width, width), width)
        for i in range(rows):
            to_cols[distance][:, i * width : (i + 1) * width] = to_rows_ref[i, from_line]
    degrees = [dot(ones[:, : cols * width], to_rows_ref[i], ((1,), (0,)))[0:1] for i in range(rows)]
    swapped = line_degrees[cols // 2 :] + line_degrees[: cols // 2]
    odd = lax.rem(here_col, 2) == 1
    for c in range(cols):
        s = c // 2 + (c % 2) * (cols // 2)
        degrees.append(jnp.where(odd, swapped[s], line_degrees[s]))
    k = picked.shape[0]
    extra = (piece_ref.shape[-2] - k) // 3
    if extra > rows + cols:
        degrees.append(jnp.zeros((extra - rows - cols, width), F32))
    left = jnp.concatenate(degrees, axis=0)
    planes = [picked.astype(BF16)]
    for _ in range(3):
        planes.append(left.astype(BF16))
        left = left - planes[-1].astype(F32)
    piece = jnp.concatenate(planes, axis=0)
    for i in range(rows):
        piece_ref[i] = piece


def product(vectors_of, parts, sizes):
    rows, cols, _ = sizes
    here_col = lax.axis_index("col")
    total = None
    for distance in range(cols):
        column = lax.rem(here_col + (cols - distance), cols)
        vectors = lanes([vectors_of(distance % 2, column // 2, i) for i in range(rows)])
        term = dot(vectors, parts[1 + distance][...], ((1,), (1,)))
        total = term if total is None else total + term
    for i in range(rows):
        vectors = lanes([vectors_of(s, x, i) for s in range(2) for x in range(cols // 2)])
        total = total + dot(vectors, parts[0][i], ((1,), (0,)))
    return total


def own_root(roots_ref):
    return roots_ref[lax.axis_index("col") // 2, pl.ds(lax.axis_index("row"), 1)]


def find_roots(sizes, k, all_ref, roots_ref):
    rows, cols, _ = sizes
    extra = (all_ref.shape[-2] - k) // 3

    def degrees(c, i):
        planes = [all_ref[c, i, k + n * extra : k + (n + 1) * extra].astype(F32) for n in range(3)]
        return (planes[0] + planes[1]) + planes[2]

    def summed(terms):
        total = terms[0]
        for term in terms[1:]:
            total = total + term
        return total

    sums = [[degrees(c, i) for i in range(rows)] for c in range(cols)]
    across = [summed([sums[c][i] for c in range(cols)]) for i in range(rows)]
    for c in range(cols):
        part = summed(sums[c])
        other = jnp.concatenate([across[i][rows + c : rows + c + 1] for i in range(rows)], axis=0)
        roots_ref[slot_of(c, cols)] = 1.0 / jnp.sqrt(part[:rows] + other)


def send(vectors, copies_ref):
    vectors = vectors.astype(BF16)
    for n in range(copies_ref.shape[0]):
        copies_ref[n] = vectors


def first_step_kernel(sizes, all_ref, picked_ref, *refs):
    rows, cols, _ = sizes
    parts, (copies_ref, own_ref, roots_ref, scratch) = refs[:-4], refs[-4:]
    k = own_ref.shape[0]
    half = cols // 2
    find_roots(sizes, k, all_ref, roots_ref)
    for c in range(cols):
        s = slot_of(c, cols)
        for i in range(rows):
            value = all_ref[c, i, :k].astype(F32) * roots_ref[s, i : i + 1]
            high = value.astype(BF16)
            scratch[s, i, :k] = high
            scratch[s, i, k:] = (value - high.astype(F32)).astype(BF16)
    total = product(lambda s, x, i: scratch[s * half + x, i], parts, sizes)
    root = own_root(roots_ref)
    image = picked_ref[...] + root * (total[:k] + total[k:])
    own_ref[...] = image
    send(root * image, copies_ref)


def next_image(sizes, same_ref, other_ref, before_ref, roots_ref, factor_ref, parts):
    half = sizes[1] // 2
    refs = (same_ref, other_ref)
    total = product(lambda s, x, i: refs[s][i * half + x], parts, sizes)
    image = before_ref[...] + own_root(roots_ref) * total
    return dot(factor_ref[...], image, ((1,), (0,)), HIGHEST)


def step_kernel(sizes, same_ref, other_ref, before_ref, roots_ref, factor_ref, *refs):
    parts, (copies_ref, own_ref) = refs[:-2], refs[-2:]
    image = next_image(sizes, same_ref, other_ref, before_ref, roots_ref, factor_ref, parts)
    own_ref[...] = image
    send(own_root(roots_ref) * image, copies_ref)


def last_step_kernel(sizes, same_ref, other_ref, before_ref, roots_ref, factor_ref, *refs):
    parts, (own_ref, gram_ref) = refs[:-2], refs[-2:]
    image = next_image(sizes, same_ref, other_ref, before_ref, roots_ref, factor_ref, parts)
    own_ref[...] = image
    gram = dot(image, image, ((1,), (1,)), HIGHEST)
    half = gram.shape[0] // 2
    gram = lanes([gram[:half], gram[half:]])
    for i in range(gram_ref.shape[0]):
        gram_ref[i] = gram


def congruent(factor, gram):
    half = dot(factor, gram, ((1,), (0,)), HIGHEST)
    return dot(half, factor, ((1,), (1,)), HIGHEST)


def first_factor_kernel(sizes, all_ref, factor_ref):
    rows, cols, _ = sizes
    k = factor_ref.shape[0]
    gram = jnp.zeros((k, k), F32)
    for c in range(cols):
        panel = lanes([all_ref[c, i, :k].astype(F32) for i in range(rows)])
        gram = gram + dot(panel, panel, ((1,), (1,)), HIGHEST)
    factor_ref[...] = inverse_factor(gram)


def factor_of(sizes, same_ref, other_ref, roots_ref, before_ref):
    rows, cols, _ = sizes
    half = cols // 2
    k = before_ref.shape[0]
    gram = jnp.zeros((k, k), F32)
    for s, ref in enumerate((same_ref, other_ref)):
        for x in range(half):
            panel = lanes([ref[i * half + x].astype(F32) / roots_ref[s * half + x, i : i + 1] for i in range(rows)])
            gram = gram + dot(panel, panel, ((1,), (1,)), HIGHEST)
    return inverse_factor(congruent(before_ref[...], gram))


def factor_kernel(sizes, same_ref, other_ref, roots_ref, before_ref, factor_ref):
    factor_ref[...] = factor_of(sizes, same_ref, other_ref, roots_ref, before_ref)


def last_factor_kernel(sizes, same_ref, other_ref, roots_ref, before_ref, image_ref, factor_ref, out_ref):
    factor = factor_of(sizes, same_ref, other_ref, roots_ref, before_ref)
    factor_ref[...] = factor
    out_ref[...] = dot(factor, image_ref[...], ((1,), (0,)), HIGHEST)


def finish_kernel(scale, grams_ref, factor_ref, image_ref, out_ref):
    packed = grams_ref[0]
    for c in range(1, grams_ref.shape[0]):
        packed = packed + grams_ref[c]
    k = factor_ref.shape[0]
    gram = jnp.concatenate([packed[:, :k], packed[:, k:]], axis=0)
    factor = inverse_factor(congruent(factor_ref[...], gram))
    out_ref[...] = scale * dot(factor, image_ref[...], ((1,), (0,)), HIGHEST)


def kernel_call(body, outs, *operands, scratch=(), space=pltpu.VMEM, limit=0):
    held = sum(math.prod(a.shape) * a.dtype.itemsize for a in (*operands, *outs))
    extra = sum(math.prod(s.shape) * 4 for s in scratch if hasattr(s, "shape"))
    spec = pl.BlockSpec(memory_space=pltpu.VMEM)
    single = len(outs) == 1
    return pl.pallas_call(
        body,
        out_shape=outs[0] if single else tuple(outs),
        in_specs=[pl.BlockSpec(memory_space=space)] * len(operands),
        out_specs=spec if single else (spec,) * len(outs),
        scratch_shapes=list(scratch),
        cost_estimate=pl.CostEstimate(flops=0, bytes_accessed=held, transcendentals=0),
        compiler_params=pltpu.CompilerParams(vmem_limit_bytes=limit or held + held // 4 + extra + (8 << 20)),
    )(*operands)


def gather_start(copies):
    return lax.all_gather(lax.all_to_all(copies, "row", 0, 0, tiled=True), "col", axis=0, tiled=False)


def gather_vectors(copies, rows, cols, factor):
    groups = [[r * cols + c for r in range(rows) for c in range(parity, cols, 2)] for parity in range(2)]
    same = lax.all_to_all(copies, ("row", "col"), 0, 0, tiled=True, axis_index_groups=groups)
    same, factor = lax.optimization_barrier((same, factor))
    return same, lax.ppermute(same, "col", [(c, c + 1 - 2 * (c % 2)) for c in range(cols)]), factor


def local(start_vectors, cluster_order, weights, block_mask):
    rows, cols = lax.axis_size("row"), lax.axis_size("col")
    k, width = start_vectors.shape
    sizes = (rows, cols, width)

    def bound(body):
        return lambda *refs: body(sizes, *refs)

    shape = jax.ShapeDtypeStruct
    extra = -(-(rows + cols) // 16) * 16
    to_rows, *to_cols, piece, picked = kernel_call(
        bound(prepare_kernel),
        [
            shape((rows, cols * width, width), BF16),
            *[shape((width, rows * width), BF16)] * cols,
            shape((rows, k + 3 * extra, width), BF16),
            shape((k, width), F32),
        ],
        block_mask[:, 0, :],
        weights[:, 0, :],
        start_vectors,
        cluster_order,
        scratch=[
            pltpu.SMEM((cols, rows), jnp.int32),
            pltpu.VMEM((cols, width, rows * width), BF16),
            pltpu.VMEM((k, width), F32),
            pltpu.VMEM((1, width), jnp.int32),
            pltpu.SemaphoreType.DMA((cols + 3,)),
        ],
        space=pltpu.HBM,
        limit=60 << 20,
    )
    everyone = gather_start(piece)
    parts = [lax.all_to_all(to_rows, "row", 0, 0, tiled=True), to_cols[0]]
    for distance in range(1, cols):
        parts.append(lax.ppermute(to_cols[distance], "col", [(c, (c + distance) % cols) for c in range(cols)]))
    copies, own_shape = shape((rows * cols // 2, k, width), BF16), shape((k, width), F32)
    factor_shape = shape((k, k), F32)
    factor = kernel_call(bound(first_factor_kernel), [factor_shape], everyone)
    everyone, factor = lax.optimization_barrier((everyone, factor))
    sent, own, roots = kernel_call(
        bound(first_step_kernel),
        [copies, own_shape, shape((cols, rows, width), F32)],
        everyone,
        picked,
        *parts,
        scratch=[pltpu.VMEM((cols, rows, 2 * k, width), BF16)],
    )
    for step in range(1, ITERS):
        same, other, factor = gather_vectors(sent, rows, cols, factor)
        if step < ITERS - 1:
            sent, own = kernel_call(
                bound(step_kernel), [copies, own_shape], same, other, own, roots, factor, *parts
            )
            factor = kernel_call(bound(factor_kernel), [factor_shape], same, other, roots, factor)
        else:
            own, gram = kernel_call(
                bound(last_step_kernel),
                [own_shape, shape((rows, k // 2, 2 * k), F32)],
                same,
                other,
                own,
                roots,
                factor,
                *parts,
            )
            factor, image = kernel_call(
                bound(last_factor_kernel), [factor_shape, own_shape], same, other, roots, factor, own
            )
    gram = lax.all_to_all(gram, "row", 0, 0, tiled=True).sum(axis=0)
    gram = lax.all_gather(gram, "col", axis=0, tiled=False)
    scale = math.sqrt(width * rows * cols)
    return kernel_call(lambda *refs: finish_kernel(scale, *refs), [own_shape], gram, factor, image)


def solution(mesh):
    placed = (
        P(None, ("row", "col")),
        P(("row", "col"), None),
        P("row", "col", None),
        P("row", "col", None),
    )
    return jax.shard_map(
        local, mesh=mesh, in_specs=placed, out_specs=P(None, ("row", "col")), check_vma=False
    )
```

```python
import math

import jax
import jax.numpy as jnp
from jax import lax
from jax.experimental import pallas as pl
from jax.experimental.pallas import tpu as pltpu
from jax.sharding import PartitionSpec as P

ITERS = 3
HIGHEST = lax.Precision.HIGHEST
F32 = jnp.float32
BF16 = jnp.bfloat16


def dot(a, b, contract, precision=None):
    return lax.dot_general(
        a, b, ((contract[0], contract[1]), ((), ())), precision=precision, preferred_element_type=F32
    )


def lanes(blocks):
    return jnp.concatenate(blocks, axis=1)


def inverse_factor(gram, tile=8):
    k = gram.shape[0]
    diagonal = lax.broadcasted_iota(jnp.int32, (k, k), 0) == lax.broadcasted_iota(jnp.int32, (k, k), 1)
    work = lanes([diagonal.astype(F32), gram])
    tiles = [work[at : at + tile] for at in range(0, k, tile)]
    row = lax.broadcasted_iota(jnp.int32, (tile, 2 * k), 0)

    def spread(part):
        return jnp.broadcast_to(part, (tile, 2 * k))

    done = []
    for b in range(len(tiles)):
        live = range(b, len(tiles))
        first = k + tile * b
        column = {
            (q, t): spread(tiles[t][:, first + q : first + q + 1]) for q in range(tile) for t in live
        }
        pivots = jnp.ones((tile, 2 * k), F32)
        for q in range(tile):
            pivot = spread(column[q, b][q : q + 1])
            pivots = jnp.where(row == q, pivot, pivots)
            inverse = 1.0 / pivot
            ratio = {t: column[q, t] * inverse for t in live}
            ratio[b] = jnp.where(row > q, ratio[b], 0.0)
            for later in range(q + 1, tile):
                entry = spread(column[later, b][q : q + 1])
                for t in live:
                    column[later, t] = column[later, t] - ratio[t] * entry
            line = spread(tiles[b][q : q + 1])
            for t in live:
                tiles[t] = tiles[t] - ratio[t] * line
        done.append((tiles[b] * (1.0 / jnp.sqrt(pivots)))[:, :k])
    return jnp.concatenate(done, axis=0)


def slots(cols):
    parity = lax.rem(lax.axis_index("col"), 2)
    return [2 * x + parity for x in range(cols // 2)] + [2 * x + 1 - parity for x in range(cols // 2)]


def slot_of(column, cols):
    other = lax.rem(column + lax.axis_index("col"), 2)
    return other * (cols // 2) + column // 2


def prepare_kernel(sizes, mask_hbm, stored_hbm, start_hbm, order_hbm, to_rows_ref, *refs):
    rows, cols, width = sizes
    to_cols, (piece_ref, picked_ref) = refs[:cols], refs[cols : cols + 2]
    mask_ref, stored_ref, start_ref, order_ref, arrived = refs[cols + 2 :]
    here_row, here_col = lax.axis_index("row"), lax.axis_index("col")
    columns = slots(cols)
    copies = [
        pltpu.make_async_copy(mask_hbm, mask_ref, arrived.at[cols]),
        pltpu.make_async_copy(start_hbm, start_ref, arrived.at[cols + 1]),
        pltpu.make_async_copy(order_hbm, order_ref, arrived.at[cols + 2]),
    ]
    lines = [
        pltpu.make_async_copy(
            stored_hbm.at[pl.ds(pl.multiple_of(columns[s] * width, width), width)], stored_ref.at[s], arrived.at[s]
        )
        for s in range(cols)
    ]
    for copy in copies + lines:
        copy.start()
    upper = (
        lax.broadcasted_iota(jnp.int32, (width, width), 0) < lax.broadcasted_iota(jnp.int32, (width, width), 1)
    ).astype(F32)
    node = lax.broadcasted_iota(jnp.int32, (width, width), 0)
    for copy in copies:
        copy.wait()
    picked = dot(start_ref[...], (node == order_ref[...]).astype(F32), ((1,), (0,)), HIGHEST)
    picked_ref[...] = picked
    ones = jnp.ones((8, rows * width), BF16)
    line_degrees = []
    for s in range(cols):
        lines[s].wait()
        row_block = here_row * cols + columns[s]
        line = []
        for i in range(rows):
            col_block = i * cols + here_col
            whole = jnp.where((mask_ref[columns[s], i] > 0) & (row_block < col_block), 1.0, 0.0)
            partly = jnp.where(row_block == col_block, 1.0, 0.0)
            keep = (whole + partly * upper).astype(BF16)
            line.append(stored_ref[s, :, i * width : (i + 1) * width] * keep)
            to_rows_ref[i, s * width : (s + 1) * width] = line[i]
        line_degrees.append(dot(ones, lanes(line), ((1,), (1,)))[0:1])
    for distance in range(cols):
        s = slot_of(lax.rem(here_col + distance, cols), cols)
        from_line = pl.ds(pl.multiple_of(s * width, width), width)
        for i in range(rows):
            to_cols[distance][:, i * width : (i + 1) * width] = to_rows_ref[i, from_line]
    degrees = [dot(ones[:, : cols * width], to_rows_ref[i], ((1,), (0,)))[0:1] for i in range(rows)]
    swapped = line_degrees[cols // 2 :] + line_degrees[: cols // 2]
    odd = lax.rem(here_col, 2) == 1
    for c in range(cols):
        s = c // 2 + (c % 2) * (cols // 2)
        degrees.append(jnp.where(odd, swapped[s], line_degrees[s]))
    k = picked.shape[0]
    extra = (piece_ref.shape[-2] - k) // 3
    if extra > rows + cols:
        degrees.append(jnp.zeros((extra - rows - cols, width), F32))
    left = jnp.concatenate(degrees, axis=0)
    planes = [picked.astype(BF16)]
    for _ in range(3):
        planes.append(left.astype(BF16))
        left = left - planes[-1].astype(F32)
    piece = jnp.concatenate(planes, axis=0)
    for i in range(rows):
        piece_ref[i] = piece


def product(vectors_of, parts, sizes):
    rows, cols, _ = sizes
    here_col = lax.axis_index("col")
    total = None
    for distance in range(cols):
        column = lax.rem(here_col + (cols - distance), cols)
        vectors = lanes([vectors_of(distance % 2, column // 2, i) for i in range(rows)])
        term = dot(vectors, parts[1 + distance][...], ((1,), (1,)))
        total = term if total is None else total + term
    for i in range(rows):
        vectors = lanes([vectors_of(s, x, i) for s in range(2) for x in range(cols // 2)])
        total = total + dot(vectors, parts[0][i], ((1,), (0,)))
    return total


def own_root(roots_ref):
    return roots_ref[lax.axis_index("col") // 2, pl.ds(lax.axis_index("row"), 1)]


def find_roots(sizes, k, all_ref, roots_ref):
    rows, cols, _ = sizes
    extra = (all_ref.shape[-2] - k) // 3

    def degrees(c, i):
        planes = [all_ref[c, i, k + n * extra : k + (n + 1) * extra].astype(F32) for n in range(3)]
        return (planes[0] + planes[1]) + planes[2]

    def summed(terms):
        total = terms[0]
        for term in terms[1:]:
            total = total + term
        return total

    sums = [[degrees(c, i) for i in range(rows)] for c in range(cols)]
    across = [summed([sums[c][i] for c in range(cols)]) for i in range(rows)]
    for c in range(cols):
        part = summed(sums[c])
        other = jnp.concatenate([across[i][rows + c : rows + c + 1] for i in range(rows)], axis=0)
        roots_ref[slot_of(c, cols)] = 1.0 / jnp.sqrt(part[:rows] + other)


def send(vectors, copies_ref):
    vectors = vectors.astype(BF16)
    for n in range(copies_ref.shape[0]):
        copies_ref[n] = vectors


def first_step_kernel(sizes, all_ref, picked_ref, *refs):
    rows, cols, _ = sizes
    parts, (copies_ref, own_ref, roots_ref, scratch) = refs[:-4], refs[-4:]
    k = own_ref.shape[0]
    half = cols // 2
    find_roots(sizes, k, all_ref, roots_ref)
    for c in range(cols):
        s = slot_of(c, cols)
        for i in range(rows):
            value = all_ref[c, i, :k].astype(F32) * roots_ref[s, i : i + 1]
            high = value.astype(BF16)
            scratch[s, i, :k] = high
            scratch[s, i, k:] = (value - high.astype(F32)).astype(BF16)
    total = product(lambda s, x, i: scratch[s * half + x, i], parts, sizes)
    root = own_root(roots_ref)
    image = picked_ref[...] + root * (total[:k] + total[k:])
    own_ref[...] = image
    send(root * image, copies_ref)


def next_image(sizes, same_ref, other_ref, before_ref, roots_ref, factor_ref, parts):
    half = sizes[1] // 2
    refs = (same_ref, other_ref)
    total = product(lambda s, x, i: refs[s][i * half + x], parts, sizes)
    image = before_ref[...] + own_root(roots_ref) * total
    return dot(factor_ref[...], image, ((1,), (0,)), HIGHEST)


def step_kernel(sizes, same_ref, other_ref, before_ref, roots_ref, factor_ref, *refs):
    parts, (copies_ref, own_ref) = refs[:-2], refs[-2:]
    image = next_image(sizes, same_ref, other_ref, before_ref, roots_ref, factor_ref, parts)
    own_ref[...] = image
    send(own_root(roots_ref) * image, copies_ref)


def last_step_kernel(sizes, same_ref, other_ref, before_ref, roots_ref, factor_ref, *refs):
    parts, (own_ref, gram_ref) = refs[:-2], refs[-2:]
    image = next_image(sizes, same_ref, other_ref, before_ref, roots_ref, factor_ref, parts)
    own_ref[...] = image
    packed = pack_gram(dot(image, image, ((1,), (1,)), HIGHEST))
    for n in range(gram_ref.shape[0]):
        gram_ref[n] = packed


def pack_gram(gram):
    half = gram.shape[0] // 2
    blocks = [gram[:half, :half], gram[half:, :half], gram[half:, half:]]
    tile = half // 4
    return jnp.concatenate([lanes([b[n * tile : (n + 1) * tile] for n in range(4)]) for b in blocks], axis=0)


def unpack_gram(packed):
    tile, half = packed.shape[0] // 3, packed.shape[1] // 4
    upper, cross, lower = [
        jnp.concatenate([packed[b * tile : (b + 1) * tile, n * half : (n + 1) * half] for n in range(4)], axis=0)
        for b in range(3)
    ]
    across = lax.transpose(cross, (1, 0))
    return jnp.concatenate([lanes([upper, across]), lanes([cross, lower])], axis=0)


def congruent(factor, gram):
    half = dot(factor, gram, ((1,), (0,)), HIGHEST)
    return dot(half, factor, ((1,), (1,)), HIGHEST)


def first_factor_kernel(sizes, all_ref, factor_ref):
    rows, cols, _ = sizes
    k = factor_ref.shape[0]
    gram = jnp.zeros((k, k), F32)
    for c in range(cols):
        panel = lanes([all_ref[c, i, :k].astype(F32) for i in range(rows)])
        gram = gram + dot(panel, panel, ((1,), (1,)), HIGHEST)
    factor_ref[...] = inverse_factor(gram)


def factor_of(sizes, same_ref, other_ref, roots_ref, before_ref):
    rows, cols, _ = sizes
    half = cols // 2
    k = before_ref.shape[0]
    gram = jnp.zeros((k, k), F32)
    for s, ref in enumerate((same_ref, other_ref)):
        for x in range(half):
            panel = lanes([ref[i * half + x].astype(F32) / roots_ref[s * half + x, i : i + 1] for i in range(rows)])
            gram = gram + dot(panel, panel, ((1,), (1,)), HIGHEST)
    return inverse_factor(congruent(before_ref[...], gram))


def factor_kernel(sizes, same_ref, other_ref, roots_ref, before_ref, factor_ref):
    factor_ref[...] = factor_of(sizes, same_ref, other_ref, roots_ref, before_ref)


def last_factor_kernel(sizes, same_ref, other_ref, roots_ref, before_ref, image_ref, factor_ref, out_ref):
    factor = factor_of(sizes, same_ref, other_ref, roots_ref, before_ref)
    factor_ref[...] = factor
    out_ref[...] = dot(factor, image_ref[...], ((1,), (0,)), HIGHEST)


def finish_kernel(scale, same_ref, other_ref, factor_ref, image_ref, out_ref):
    gram = unpack_gram(same_ref[...] + other_ref[...])
    factor = inverse_factor(congruent(factor_ref[...], gram))
    out_ref[...] = scale * dot(factor, image_ref[...], ((1,), (0,)), HIGHEST)


def kernel_call(body, outs, *operands, scratch=(), space=pltpu.VMEM, limit=0):
    held = sum(math.prod(a.shape) * a.dtype.itemsize for a in (*operands, *outs))
    extra = sum(math.prod(s.shape) * 4 for s in scratch if hasattr(s, "shape"))
    spec = pl.BlockSpec(memory_space=pltpu.VMEM)
    single = len(outs) == 1
    return pl.pallas_call(
        body,
        out_shape=outs[0] if single else tuple(outs),
        in_specs=[pl.BlockSpec(memory_space=space)] * len(operands),
        out_specs=spec if single else (spec,) * len(outs),
        scratch_shapes=list(scratch),
        cost_estimate=pl.CostEstimate(flops=0, bytes_accessed=held, transcendentals=0),
        compiler_params=pltpu.CompilerParams(vmem_limit_bytes=limit or held + held // 4 + extra + (8 << 20)),
    )(*operands)


def gather_start(copies):
    return lax.all_gather(lax.all_to_all(copies, "row", 0, 0, tiled=True), "col", axis=0, tiled=False)


def parities(rows, cols):
    return [[r * cols + c for r in range(rows) for c in range(parity, cols, 2)] for parity in range(2)]


def swap(cols):
    return [(c, c + 1 - 2 * (c % 2)) for c in range(cols)]


def gather_vectors(copies, rows, cols, factor):
    same = lax.all_to_all(copies, ("row", "col"), 0, 0, tiled=True, axis_index_groups=parities(rows, cols))
    same, factor = lax.optimization_barrier((same, factor))
    return same, lax.ppermute(same, "col", swap(cols)), factor


def local(start_vectors, cluster_order, weights, block_mask):
    rows, cols = lax.axis_size("row"), lax.axis_size("col")
    k, width = start_vectors.shape
    sizes = (rows, cols, width)

    def bound(body):
        return lambda *refs: body(sizes, *refs)

    shape = jax.ShapeDtypeStruct
    extra = -(-(rows + cols) // 16) * 16
    to_rows, *to_cols, piece, picked = kernel_call(
        bound(prepare_kernel),
        [
            shape((rows, cols * width, width), BF16),
            *[shape((width, rows * width), BF16)] * cols,
            shape((rows, k + 3 * extra, width), BF16),
            shape((k, width), F32),
        ],
        block_mask[:, 0, :],
        weights[:, 0, :],
        start_vectors,
        cluster_order,
        scratch=[
            pltpu.SMEM((cols, rows), jnp.int32),
            pltpu.VMEM((cols, width, rows * width), BF16),
            pltpu.VMEM((k, width), F32),
            pltpu.VMEM((1, width), jnp.int32),
            pltpu.SemaphoreType.DMA((cols + 3,)),
        ],
        space=pltpu.HBM,
        limit=60 << 20,
    )
    everyone = gather_start(piece)
    parts = [lax.all_to_all(to_rows, "row", 0, 0, tiled=True), to_cols[0]]
    for distance in range(1, cols):
        parts.append(lax.ppermute(to_cols[distance], "col", [(c, (c + distance) % cols) for c in range(cols)]))
    copies, own_shape = shape((rows * cols // 2, k, width), BF16), shape((k, width), F32)
    factor_shape = shape((k, k), F32)
    factor = kernel_call(bound(first_factor_kernel), [factor_shape], everyone)
    everyone, factor = lax.optimization_barrier((everyone, factor))
    sent, own, roots = kernel_call(
        bound(first_step_kernel),
        [copies, own_shape, shape((cols, rows, width), F32)],
        everyone,
        picked,
        *parts,
        scratch=[pltpu.VMEM((cols, rows, 2 * k, width), BF16)],
    )
    for step in range(1, ITERS):
        same, other, factor = gather_vectors(sent, rows, cols, factor)
        if step < ITERS - 1:
            sent, own = kernel_call(
                bound(step_kernel), [copies, own_shape], same, other, own, roots, factor, *parts
            )
            factor = kernel_call(bound(factor_kernel), [factor_shape], same, other, roots, factor)
        else:
            own, gram = kernel_call(
                bound(last_step_kernel),
                [own_shape, shape((rows * cols // 2, 3 * k // 8, 2 * k), F32)],
                same,
                other,
                own,
                roots,
                factor,
                *parts,
            )
            factor, image = kernel_call(
                bound(last_factor_kernel), [factor_shape, own_shape], same, other, roots, factor, own
            )
    gram = lax.all_to_all(gram, ("row", "col"), 0, 0, tiled=True, axis_index_groups=parities(rows, cols))
    gram, factor = lax.optimization_barrier((gram, factor))
    same = gram.sum(axis=0)
    other = lax.ppermute(same, "col", swap(cols))
    scale = math.sqrt(width * rows * cols)
    return kernel_call(lambda *refs: finish_kernel(scale, *refs), [own_shape], same, other, factor, image)


def solution(mesh):
    placed = (
        P(None, ("row", "col")),
        P(("row", "col"), None),
        P("row", "col", None),
        P("row", "col", None),
    )
    return jax.shard_map(
        local, mesh=mesh, in_specs=placed, out_specs=P(None, ("row", "col")), check_vma=False
    )
```

```python
import math

import jax
import jax.numpy as jnp
from jax import lax
from jax.experimental import pallas as pl
from jax.experimental.pallas import tpu as pltpu
from jax.sharding import PartitionSpec as P

ITERS = 3
PLANES = 3
HIGHEST = lax.Precision.HIGHEST
F32 = jnp.float32
BF16 = jnp.bfloat16


def dot(a, b, contract, precision=None):
    return lax.dot_general(
        a, b, ((contract[0], contract[1]), ((), ())), precision=precision, preferred_element_type=F32
    )


def lanes(blocks):
    return jnp.concatenate(blocks, axis=1)


def inverse_factor(gram, tile=8):
    k = gram.shape[0]
    diagonal = lax.broadcasted_iota(jnp.int32, (k, k), 0) == lax.broadcasted_iota(jnp.int32, (k, k), 1)
    work = lanes([diagonal.astype(F32), gram])
    tiles = [work[at : at + tile] for at in range(0, k, tile)]
    row = lax.broadcasted_iota(jnp.int32, (tile, 2 * k), 0)

    def spread(part):
        return jnp.broadcast_to(part, (tile, 2 * k))

    done = []
    for b in range(len(tiles)):
        live = range(b, len(tiles))
        first = k + tile * b
        column = {
            (q, t): spread(tiles[t][:, first + q : first + q + 1]) for q in range(tile) for t in live
        }
        pivots = jnp.ones((tile, 2 * k), F32)
        for q in range(tile):
            pivot = spread(column[q, b][q : q + 1])
            pivots = jnp.where(row == q, pivot, pivots)
            inverse = 1.0 / pivot
            ratio = {t: column[q, t] * inverse for t in live}
            ratio[b] = jnp.where(row > q, ratio[b], 0.0)
            for later in range(q + 1, tile):
                entry = spread(column[later, b][q : q + 1])
                for t in live:
                    column[later, t] = column[later, t] - ratio[t] * entry
            line = spread(tiles[b][q : q + 1])
            for t in live:
                tiles[t] = tiles[t] - ratio[t] * line
        done.append((tiles[b] * (1.0 / jnp.sqrt(pivots)))[:, :k])
    return jnp.concatenate(done, axis=0)


def slots(cols):
    parity = lax.rem(lax.axis_index("col"), 2)
    return [2 * x + parity for x in range(cols // 2)] + [2 * x + 1 - parity for x in range(cols // 2)]


def slot_of(column, cols):
    other = lax.rem(column + lax.axis_index("col"), 2)
    return other * (cols // 2) + column // 2


def prepare_kernel(sizes, mask_hbm, stored_hbm, start_hbm, order_hbm, *refs):
    rows, cols, width = sizes
    to_rows, to_cols_ref = refs[:rows], refs[rows]
    piece_ref, picked_ref, mask_ref, stored_ref, start_ref, order_ref, sums_ref, arrived = refs[rows + 1 :]
    here_row, here_col = lax.axis_index("row"), lax.axis_index("col")
    columns = slots(cols)
    copies = [
        pltpu.make_async_copy(mask_hbm, mask_ref, arrived.at[cols]),
        pltpu.make_async_copy(start_hbm, start_ref, arrived.at[cols + 1]),
        pltpu.make_async_copy(order_hbm, order_ref, arrived.at[cols + 2]),
    ]
    lines = [
        pltpu.make_async_copy(
            stored_hbm.at[pl.ds(pl.multiple_of(columns[s] * width, width), width)], stored_ref.at[s], arrived.at[s]
        )
        for s in range(cols)
    ]
    for copy in copies + lines:
        copy.start()
    upper = (
        lax.broadcasted_iota(jnp.int32, (width, width), 0) < lax.broadcasted_iota(jnp.int32, (width, width), 1)
    ).astype(F32)
    node = lax.broadcasted_iota(jnp.int32, (width, width), 0)
    for copy in copies:
        copy.wait()
    picked = dot(start_ref[...], (node == order_ref[...]).astype(F32), ((1,), (0,)), HIGHEST)
    picked_ref[...] = picked
    ones = jnp.ones((8, rows * width), BF16)
    line_degrees = []
    for s in range(cols):
        lines[s].wait()
        row_block = here_row * cols + columns[s]
        line = []
        for distance in range(rows):
            i = lax.rem(here_row + distance, rows)
            col_block = i * cols + here_col
            whole = jnp.where((mask_ref[columns[s], i] > 0) & (row_block < col_block), 1.0, 0.0)
            partly = jnp.where(row_block == col_block, 1.0, 0.0)
            keep = (whole + partly * upper).astype(BF16)
            line.append(stored_ref[s, :, pl.ds(pl.multiple_of(i * width, width), width)] * keep)
            to_rows[distance][s * width : (s + 1) * width] = line[-1]
            to_cols_ref[columns[s], :, distance * width : (distance + 1) * width] = line[-1]
        line_degrees.append(dot(ones, lanes(line), ((1,), (1,)))[0:1])
    for distance in range(rows):
        part = dot(ones[:, : cols * width], to_rows[distance][...], ((1,), (0,)))
        sums_ref[pl.ds(lax.rem(here_row + distance, rows), 1)] = part[0:1]
    degrees = [sums_ref[...]]
    swapped = line_degrees[cols // 2 :] + line_degrees[: cols // 2]
    odd = lax.rem(here_col, 2) == 1
    for c in range(cols):
        s = c // 2 + (c % 2) * (cols // 2)
        degrees.append(jnp.where(odd, swapped[s], line_degrees[s]))
    k = picked.shape[0]
    extra = (piece_ref.shape[-2] - k) // PLANES
    if extra > rows + cols:
        degrees.append(jnp.zeros((extra - rows - cols, width), F32))
    left = jnp.concatenate(degrees, axis=0)
    planes = [picked.astype(BF16)]
    for _ in range(PLANES):
        planes.append(left.astype(BF16))
        left = left - planes[-1].astype(F32)
    piece = jnp.concatenate(planes, axis=0)
    piece_ref[...] = piece


def product(vectors_of, parts, sizes):
    rows, cols, _ = sizes
    here_row, here_col = lax.axis_index("row"), lax.axis_index("col")
    total = None
    for distance in range(cols):
        column = lax.rem(here_col + (cols - distance), cols)
        sources = [lax.rem(here_row + i, rows) for i in range(rows)]
        vectors = lanes([vectors_of(distance % 2, column // 2, i) for i in sources])
        term = dot(vectors, parts[rows][column], ((1,), (1,)))
        total = term if total is None else total + term
    for distance in range(rows):
        i = lax.rem(here_row + (rows - distance), rows)
        vectors = lanes([vectors_of(s, x, i) for s in range(2) for x in range(cols // 2)])
        total = total + dot(vectors, parts[distance][...], ((1,), (0,)))
    return total


def own_root(roots_ref):
    return roots_ref[lax.axis_index("col") // 2, pl.ds(lax.axis_index("row"), 1)]


def slot_rows(rows):
    here = lax.axis_index("row")
    found = []
    for distance in range(0, rows, 2):
        row = lax.rem(here + (rows - distance), rows)
        found += [row, row + 1 - 2 * lax.rem(row, 2)]
    return found


def find_roots(sizes, k, all_ref, roots_ref):
    rows, cols, _ = sizes
    extra = (all_ref.shape[-2] - k) // PLANES

    def degrees(c, i):
        planes = [all_ref[c, i, k + n * extra : k + (n + 1) * extra].astype(F32) for n in range(PLANES)]
        return (planes[0] + planes[1]) + planes[2]

    def summed(terms):
        total = terms[0]
        for term in terms[1:]:
            total = total + term
        return total

    sums = [[degrees(c, i) for i in range(rows)] for c in range(cols)]
    across = [summed([sums[c][n] for c in range(cols)]) for n in range(rows)]
    for c in range(cols):
        s = slot_of(c, cols)
        for n, place in enumerate(slot_rows(rows)):
            roots_ref[s, pl.ds(place, 1)] = across[n][rows + c : rows + c + 1]
        roots_ref[s] = 1.0 / jnp.sqrt(roots_ref[s] + summed(sums[c])[:rows])


def send(vectors, copies_ref):
    vectors = vectors.astype(BF16)
    for n in range(copies_ref.shape[0]):
        copies_ref[n] = vectors


def first_step_kernel(sizes, all_ref, picked_ref, *refs):
    rows, cols, _ = sizes
    parts, (copies_ref, own_ref, roots_ref, scratch) = refs[:-4], refs[-4:]
    k = own_ref.shape[0]
    half = cols // 2
    find_roots(sizes, k, all_ref, roots_ref)
    for c in range(cols):
        s = slot_of(c, cols)
        for n, place in enumerate(slot_rows(rows)):
            value = all_ref[c, n, :k].astype(F32) * roots_ref[s, pl.ds(place, 1)]
            high = value.astype(BF16)
            scratch[s, place, :k] = high
            scratch[s, place, k:] = (value - high.astype(F32)).astype(BF16)
    total = product(lambda s, x, i: scratch[s * half + x, i], parts, sizes)
    root = own_root(roots_ref)
    image = picked_ref[...] + root * (total[:k] + total[k:])
    own_ref[...] = image
    send(root * image, copies_ref)


def next_image(sizes, same_ref, other_ref, before_ref, roots_ref, factor_ref, parts):
    half = sizes[1] // 2
    refs = (same_ref, other_ref)
    total = product(lambda s, x, i: refs[s][i * half + x], parts, sizes)
    image = before_ref[...] + own_root(roots_ref) * total
    return dot(factor_ref[...], image, ((1,), (0,)), HIGHEST)


def step_kernel(sizes, same_ref, other_ref, before_ref, roots_ref, factor_ref, *refs):
    parts, (copies_ref, own_ref) = refs[:-2], refs[-2:]
    image = next_image(sizes, same_ref, other_ref, before_ref, roots_ref, factor_ref, parts)
    own_ref[...] = image
    send(own_root(roots_ref) * image, copies_ref)


def last_step_kernel(sizes, same_ref, other_ref, before_ref, roots_ref, factor_ref, *refs):
    parts, (own_ref, gram_ref) = refs[:-2], refs[-2:]
    image = next_image(sizes, same_ref, other_ref, before_ref, roots_ref, factor_ref, parts)
    own_ref[...] = image
    packed = pack_gram(dot(image, image, ((1,), (1,)), HIGHEST))
    for n in range(gram_ref.shape[0]):
        gram_ref[n] = packed


def pack_gram(gram):
    half = gram.shape[0] // 2
    blocks = [gram[:half, :half], gram[half:, :half], gram[half:, half:]]
    tile = half // 4
    return jnp.concatenate([lanes([b[n * tile : (n + 1) * tile] for n in range(4)]) for b in blocks], axis=0)


def unpack_gram(packed):
    tile, half = packed.shape[0] // 3, packed.shape[1] // 4
    upper, cross, lower = [
        jnp.concatenate([packed[b * tile : (b + 1) * tile, n * half : (n + 1) * half] for n in range(4)], axis=0)
        for b in range(3)
    ]
    across = lax.transpose(cross, (1, 0))
    return jnp.concatenate([lanes([upper, across]), lanes([cross, lower])], axis=0)


def congruent(factor, gram):
    half = dot(factor, gram, ((1,), (0,)), HIGHEST)
    return dot(half, factor, ((1,), (1,)), HIGHEST)


def first_factor_kernel(sizes, all_ref, factor_ref):
    rows, cols, _ = sizes
    k = factor_ref.shape[0]
    gram = jnp.zeros((k, k), F32)
    for c in range(cols):
        panel = lanes([all_ref[c, i, :k].astype(F32) for i in range(rows)])
        gram = gram + dot(panel, panel, ((1,), (1,)), HIGHEST)
    factor_ref[...] = inverse_factor(gram)


def factor_of(sizes, same_ref, other_ref, roots_ref, before_ref):
    rows, cols, _ = sizes
    half = cols // 2
    k = before_ref.shape[0]
    gram = jnp.zeros((k, k), F32)
    for s, ref in enumerate((same_ref, other_ref)):
        for x in range(half):
            panel = lanes([ref[i * half + x].astype(F32) / roots_ref[s * half + x, i : i + 1] for i in range(rows)])
            gram = gram + dot(panel, panel, ((1,), (1,)), HIGHEST)
    return inverse_factor(congruent(before_ref[...], gram))


def factor_kernel(sizes, same_ref, other_ref, roots_ref, before_ref, factor_ref):
    factor_ref[...] = factor_of(sizes, same_ref, other_ref, roots_ref, before_ref)


def last_factor_kernel(sizes, same_ref, other_ref, roots_ref, before_ref, image_ref, factor_ref, out_ref):
    factor = factor_of(sizes, same_ref, other_ref, roots_ref, before_ref)
    factor_ref[...] = factor
    out_ref[...] = dot(factor, image_ref[...], ((1,), (0,)), HIGHEST)


def finish_kernel(scale, same_ref, other_ref, factor_ref, image_ref, out_ref):
    gram = unpack_gram(same_ref[...] + other_ref[...])
    factor = inverse_factor(congruent(factor_ref[...], gram))
    out_ref[...] = scale * dot(factor, image_ref[...], ((1,), (0,)), HIGHEST)


def kernel_call(body, outs, *operands, scratch=(), space=pltpu.VMEM, limit=0):
    held = sum(math.prod(a.shape) * a.dtype.itemsize for a in (*operands, *outs))
    extra = sum(math.prod(s.shape) * 4 for s in scratch if hasattr(s, "shape"))
    spec = pl.BlockSpec(memory_space=pltpu.VMEM)
    single = len(outs) == 1
    return pl.pallas_call(
        body,
        out_shape=outs[0] if single else tuple(outs),
        in_specs=[pl.BlockSpec(memory_space=space)] * len(operands),
        out_specs=spec if single else (spec,) * len(outs),
        scratch_shapes=list(scratch),
        cost_estimate=pl.CostEstimate(flops=0, bytes_accessed=held, transcendentals=0),
        compiler_params=pltpu.CompilerParams(vmem_limit_bytes=limit or held + held // 4 + extra + (8 << 20)),
    )(*operands)


def pass_start(piece, rows):
    pieces = jnp.stack([piece, lax.ppermute(piece, "row", [(i, i + 1 - 2 * (i % 2)) for i in range(rows)])])
    return [pieces] + [
        lax.ppermute(pieces, "row", [(i, (i + distance) % rows) for i in range(rows)])
        for distance in range(2, rows, 2)
    ]


def parities(rows, cols):
    return [[r * cols + c for r in range(rows) for c in range(parity, cols, 2)] for parity in range(2)]


def swap(cols):
    return [(c, c + 1 - 2 * (c % 2)) for c in range(cols)]


def gather_vectors(copies, rows, cols, factor):
    same = lax.all_to_all(copies, ("row", "col"), 0, 0, tiled=True, axis_index_groups=parities(rows, cols))
    same, factor = lax.optimization_barrier((same, factor))
    return same, lax.ppermute(same, "col", swap(cols)), factor


def move_up(part, rows, distance):
    return lax.ppermute(part, "row", [(i, i + distance) for i in range(rows - distance)])


def exchange(parts, rows, cols, near):
    parts = list(parts)
    for distance in range(near + 1, rows):
        parts[distance] = move_up(parts[distance], rows, distance)
    parts[rows] = lax.all_to_all(parts[rows], "col", 0, 0, tiled=True)
    return parts


def local(start_vectors, cluster_order, weights, block_mask):
    rows, cols = lax.axis_size("row"), lax.axis_size("col")
    k, width = start_vectors.shape
    sizes = (rows, cols, width)

    def bound(body):
        return lambda *refs: body(sizes, *refs)

    shape = jax.ShapeDtypeStruct
    extra = -(-(rows + cols) // 16) * 16
    *parts, piece, picked = kernel_call(
        bound(prepare_kernel),
        [
            *[shape((cols * width, width), BF16)] * rows,
            shape((cols, width, rows * width), BF16),
            shape((k + PLANES * extra, width), BF16),
            shape((k, width), F32),
        ],
        block_mask[:, 0, :],
        weights[:, 0, :],
        start_vectors,
        cluster_order,
        scratch=[
            pltpu.SMEM((cols, rows), jnp.int32),
            pltpu.VMEM((cols, width, rows * width), BF16),
            pltpu.VMEM((k, width), F32),
            pltpu.VMEM((1, width), jnp.int32),
            pltpu.VMEM((rows, width), F32),
            pltpu.SemaphoreType.DMA((cols + 3,)),
        ],
        space=pltpu.HBM,
        limit=60 << 20,
    )
    groups = pass_start(piece, rows)
    parts = list(parts)
    groups[0], *tied = lax.optimization_barrier([groups[0], *parts[1:rows]])
    parts[1:rows] = tied
    near = 2
    parts = exchange(parts, rows, cols, near)
    everyone = lax.all_gather(jnp.concatenate(groups), "col", axis=0, tiled=False)
    everyone, *tied = lax.optimization_barrier([everyone, *parts[1 : near + 1]])
    parts[1 : near + 1] = [move_up(part, rows, 1 + n) for n, part in enumerate(tied)]
    copies, own_shape = shape((rows * cols // 2, k, width), BF16), shape((k, width), F32)
    factor_shape = shape((k, k), F32)
    factor = kernel_call(bound(first_factor_kernel), [factor_shape], everyone)
    everyone, factor = lax.optimization_barrier((everyone, factor))
    sent, own, roots = kernel_call(
        bound(first_step_kernel),
        [copies, own_shape, shape((cols, rows, width), F32)],
        everyone,
        picked,
        *parts,
        scratch=[pltpu.VMEM((cols, rows, 2 * k, width), BF16)],
    )
    for step in range(1, ITERS):
        same, other, factor = gather_vectors(sent, rows, cols, factor)
        if step < ITERS - 1:
            sent, own = kernel_call(
                bound(step_kernel), [copies, own_shape], same, other, own, roots, factor, *parts
            )
            factor = kernel_call(bound(factor_kernel), [factor_shape], same, other, roots, factor)
        else:
            own, gram = kernel_call(
                bound(last_step_kernel),
                [own_shape, shape((rows * cols // 2, 3 * k // 8, 2 * k), F32)],
                same,
                other,
                own,
                roots,
                factor,
                *parts,
            )
            factor, image = kernel_call(
                bound(last_factor_kernel), [factor_shape, own_shape], same, other, roots, factor, own
            )
    gram = lax.all_to_all(gram, ("row", "col"), 0, 0, tiled=True, axis_index_groups=parities(rows, cols))
    gram, factor = lax.optimization_barrier((gram, factor))
    same = gram.sum(axis=0)
    other = lax.ppermute(same, "col", swap(cols))
    scale = math.sqrt(width * rows * cols)
    return kernel_call(lambda *refs: finish_kernel(scale, *refs), [own_shape], same, other, factor, image)


def solution(mesh):
    placed = (
        P(None, ("row", "col")),
        P(("row", "col"), None),
        P("row", "col", None),
        P("row", "col", None),
    )
    return jax.shard_map(
        local, mesh=mesh, in_specs=placed, out_specs=P(None, ("row", "col")), check_vma=False
    )
```

```python
import math

import jax
import jax.numpy as jnp
from jax import lax
from jax.experimental import pallas as pl
from jax.experimental.pallas import tpu as pltpu
from jax.sharding import PartitionSpec as P

ITERS = 3
HIGHEST = lax.Precision.HIGHEST
F32 = jnp.float32
BF16 = jnp.bfloat16


def dot(a, b, contract, precision=None):
    return lax.dot_general(
        a, b, ((contract[0], contract[1]), ((), ())), precision=precision, preferred_element_type=F32
    )


def lanes(blocks):
    return jnp.concatenate(blocks, axis=1)


def inverse_factor(gram, tile=8):
    k = gram.shape[0]
    diagonal = lax.broadcasted_iota(jnp.int32, (k, k), 0) == lax.broadcasted_iota(jnp.int32, (k, k), 1)
    work = lanes([diagonal.astype(F32), gram])
    tiles = [work[at : at + tile] for at in range(0, k, tile)]
    row = lax.broadcasted_iota(jnp.int32, (tile, 2 * k), 0)

    def spread(part):
        return jnp.broadcast_to(part, (tile, 2 * k))

    done = []
    for b in range(len(tiles)):
        live = range(b, len(tiles))
        first = k + tile * b
        column = {
            (q, t): spread(tiles[t][:, first + q : first + q + 1]) for q in range(tile) for t in live
        }
        pivots = jnp.ones((tile, 2 * k), F32)
        for q in range(tile):
            pivot = spread(column[q, b][q : q + 1])
            pivots = jnp.where(row == q, pivot, pivots)
            inverse = 1.0 / pivot
            ratio = {t: column[q, t] * inverse for t in live}
            ratio[b] = jnp.where(row > q, ratio[b], 0.0)
            for later in range(q + 1, tile):
                entry = spread(column[later, b][q : q + 1])
                for t in live:
                    column[later, t] = column[later, t] - ratio[t] * entry
            line = spread(tiles[b][q : q + 1])
            for t in live:
                tiles[t] = tiles[t] - ratio[t] * line
        done.append((tiles[b] * (1.0 / jnp.sqrt(pivots)))[:, :k])
    return jnp.concatenate(done, axis=0)


def slots(cols):
    parity = lax.rem(lax.axis_index("col"), 2)
    return [2 * x + parity for x in range(cols // 2)] + [2 * x + 1 - parity for x in range(cols // 2)]


def slot_of(column, cols):
    other = lax.rem(column + lax.axis_index("col"), 2)
    return other * (cols // 2) + column // 2


def prepare_kernel(sizes, mask_hbm, stored_hbm, start_hbm, order_hbm, to_rows_ref, *refs):
    rows, cols, width = sizes
    to_cols, (piece_ref, picked_ref) = refs[:cols], refs[cols : cols + 2]
    mask_ref, stored_ref, start_ref, order_ref, arrived = refs[cols + 2 :]
    here_row, here_col = lax.axis_index("row"), lax.axis_index("col")
    columns = slots(cols)
    copies = [
        pltpu.make_async_copy(mask_hbm, mask_ref, arrived.at[cols]),
        pltpu.make_async_copy(start_hbm, start_ref, arrived.at[cols + 1]),
        pltpu.make_async_copy(order_hbm, order_ref, arrived.at[cols + 2]),
    ]
    lines = [
        pltpu.make_async_copy(
            stored_hbm.at[pl.ds(pl.multiple_of(columns[s] * width, width), width)], stored_ref.at[s], arrived.at[s]
        )
        for s in range(cols)
    ]
    for copy in copies + lines:
        copy.start()
    upper = (
        lax.broadcasted_iota(jnp.int32, (width, width), 0) < lax.broadcasted_iota(jnp.int32, (width, width), 1)
    ).astype(F32)
    node = lax.broadcasted_iota(jnp.int32, (width, width), 0)
    for copy in copies:
        copy.wait()
    picked = dot(start_ref[...], (node == order_ref[...]).astype(F32), ((1,), (0,)), HIGHEST)
    picked_ref[...] = picked
    ones = jnp.ones((8, rows * width), BF16)
    line_degrees = []
    for s in range(cols):
        lines[s].wait()
        row_block = here_row * cols + columns[s]
        line = []
        for i in range(rows):
            col_block = i * cols + here_col
            whole = jnp.where((mask_ref[columns[s], i] > 0) & (row_block < col_block), 1.0, 0.0)
            partly = jnp.where(row_block == col_block, 1.0, 0.0)
            keep = (whole + partly * upper).astype(BF16)
            line.append(stored_ref[s, :, i * width : (i + 1) * width] * keep)
            to_rows_ref[i, s * width : (s + 1) * width] = line[i]
        line_degrees.append(dot(ones, lanes(line), ((1,), (1,)))[0:1])
    for distance in range(cols):
        s = slot_of(lax.rem(here_col + distance, cols), cols)
        from_line = pl.ds(pl.multiple_of(s * width, width), width)
        for i in range(rows):
            to_cols[distance][:, i * width : (i + 1) * width] = to_rows_ref[i, from_line]
    degrees = [dot(ones[:, : cols * width], to_rows_ref[i], ((1,), (0,)))[0:1] for i in range(rows)]
    swapped = line_degrees[cols // 2 :] + line_degrees[: cols // 2]
    odd = lax.rem(here_col, 2) == 1
    for c in range(cols):
        s = c // 2 + (c % 2) * (cols // 2)
        degrees.append(jnp.where(odd, swapped[s], line_degrees[s]))
    k = picked.shape[0]
    spare = piece_ref.shape[-2] - k - rows - cols
    if spare:
        degrees.append(jnp.zeros((spare, width), F32))
    degrees = jnp.concatenate(degrees, axis=0)
    for i in range(rows):
        piece_ref[i, :k] = picked
        piece_ref[i, k:] = degrees


def product(vectors_of, parts, sizes):
    rows, cols, _ = sizes
    here_col = lax.axis_index("col")
    total = None
    for distance in range(cols):
        column = lax.rem(here_col + (cols - distance), cols)
        vectors = lanes([vectors_of(distance % 2, column // 2, i) for i in range(rows)])
        term = dot(vectors, parts[1 + distance][...], ((1,), (1,)))
        total = term if total is None else total + term
    for i in range(rows):
        vectors = lanes([vectors_of(s, x, i) for s in range(2) for x in range(cols // 2)])
        total = total + dot(vectors, parts[0][i], ((1,), (0,)))
    return total


def own_root(roots_ref):
    return roots_ref[lax.axis_index("col") // 2, pl.ds(lax.axis_index("row"), 1)]


def find_roots(sizes, k, block_of, roots_ref):
    rows, cols, _ = sizes

    def summed(terms):
        total = terms[0]
        for term in terms[1:]:
            total = total + term
        return total

    sums = [[block_of(c, i)[k:] for i in range(rows)] for c in range(cols)]
    across = [summed([sums[c][i] for c in range(cols)]) for i in range(rows)]
    for c in range(cols):
        part = summed(sums[c])
        other = jnp.concatenate([across[i][rows + c : rows + c + 1] for i in range(rows)], axis=0)
        roots_ref[slot_of(c, cols)] = 1.0 / jnp.sqrt(part[:rows] + other)


def send(value, copies_ref):
    for n in range(copies_ref.shape[0]):
        copies_ref[n] = value


def panel_gram(panels):
    gram = None
    for panel in panels:
        term = dot(panel, panel, ((1,), (1,)), HIGHEST)
        gram = term if gram is None else gram + term
    return gram


def start_kernel(sizes, low_ref, high_ref, picked_ref, vectors_ref, own_ref, roots_ref):
    rows, cols, width = sizes
    k = own_ref.shape[0]
    half = low_ref.shape[1]

    def block_of(c, i):
        return low_ref.at[c, i] if i < half else high_ref.at[c, i - half]

    find_roots(sizes, k, block_of, roots_ref)

    def panel_of(c):
        return lanes([block_of(c, i)[:k] for i in range(rows)])

    factor = inverse_factor(panel_gram([panel_of(c) for c in range(cols)]))
    for c in range(cols):
        s = slot_of(c, cols)
        panel = dot(factor, panel_of(c), ((1,), (0,)), HIGHEST)
        for i in range(rows):
            vectors_ref[s, i] = (roots_ref[s, i : i + 1] * panel[:, i * width : (i + 1) * width]).astype(BF16)
    own_ref[...] = dot(factor, picked_ref[...], ((1,), (0,)), HIGHEST)


def first_step_kernel(sizes, vectors_ref, own_ref, roots_ref, *refs):
    parts, copies_ref = refs[:-1], refs[-1]
    half = sizes[1] // 2
    total = product(lambda s, x, i: vectors_ref[s * half + x, i], parts, sizes)
    send(own_ref[...] + own_root(roots_ref) * total, copies_ref)


def half_gram_kernel(sizes, same_ref, gram_ref):
    rows, cols, _ = sizes
    half = cols // 2
    gram_ref[...] = panel_gram([lanes([same_ref[i * half + x] for i in range(rows)]) for x in range(half)])


def next_image(sizes, same_ref, other_ref, gram_ref, roots_ref, parts, scratch):
    rows, cols, width = sizes
    half = cols // 2
    refs = (same_ref, other_ref)

    def panel_of(s, x):
        return lanes([refs[s][i * half + x] for i in range(rows)])

    factor = inverse_factor(gram_ref[...] + panel_gram([panel_of(1, x) for x in range(half)]))
    for s in range(2):
        for x in range(half):
            panel = dot(factor, panel_of(s, x), ((1,), (0,)), HIGHEST)
            for i in range(rows):
                root = roots_ref[s * half + x, i : i + 1]
                scratch[s * half + x, i] = (root * panel[:, i * width : (i + 1) * width]).astype(BF16)
    total = product(lambda s, x, i: scratch[s * half + x, i], parts, sizes)
    here = lax.axis_index("row") * half + lax.axis_index("col") // 2
    return dot(factor, same_ref[here], ((1,), (0,)), HIGHEST) + own_root(roots_ref) * total


def step_kernel(sizes, same_ref, other_ref, gram_ref, roots_ref, *refs):
    parts, (copies_ref, scratch) = refs[:-2], refs[-2:]
    send(next_image(sizes, same_ref, other_ref, gram_ref, roots_ref, parts, scratch), copies_ref)


def last_step_kernel(sizes, same_ref, other_ref, gram_ref, roots_ref, *refs):
    parts, (own_ref, grams_ref, scratch) = refs[:-3], refs[-3:]
    image = next_image(sizes, same_ref, other_ref, gram_ref, roots_ref, parts, scratch)
    own_ref[...] = image
    send(pack_gram(dot(image, image, ((1,), (1,)), HIGHEST)), grams_ref)


def pack_gram(gram):
    half = gram.shape[0] // 2
    blocks = [gram[:half, :half], gram[half:, :half], gram[half:, half:]]
    tile = half // 4
    return jnp.concatenate([lanes([b[n * tile : (n + 1) * tile] for n in range(4)]) for b in blocks], axis=0)


def unpack_gram(packed):
    tile, half = packed.shape[0] // 3, packed.shape[1] // 4
    upper, cross, lower = [
        jnp.concatenate([packed[b * tile : (b + 1) * tile, n * half : (n + 1) * half] for n in range(4)], axis=0)
        for b in range(3)
    ]
    across = lax.transpose(cross, (1, 0))
    return jnp.concatenate([lanes([upper, across]), lanes([cross, lower])], axis=0)


def finish_kernel(scale, same_ref, other_ref, image_ref, out_ref):
    factor = inverse_factor(unpack_gram(same_ref[...] + other_ref[...]))
    out_ref[...] = scale * dot(factor, image_ref[...], ((1,), (0,)), HIGHEST)


def kernel_call(body, outs, *operands, scratch=(), space=pltpu.VMEM, limit=0):
    held = sum(math.prod(a.shape) * a.dtype.itemsize for a in (*operands, *outs))
    extra = sum(math.prod(s.shape) * 4 for s in scratch if hasattr(s, "shape"))
    spec = pl.BlockSpec(memory_space=pltpu.VMEM)
    single = len(outs) == 1
    return pl.pallas_call(
        body,
        out_shape=outs[0] if single else tuple(outs),
        in_specs=[pl.BlockSpec(memory_space=space)] * len(operands),
        out_specs=spec if single else (spec,) * len(outs),
        scratch_shapes=list(scratch),
        cost_estimate=pl.CostEstimate(flops=0, bytes_accessed=held, transcendentals=0),
        compiler_params=pltpu.CompilerParams(vmem_limit_bytes=limit or held + held // 4 + extra + (8 << 20)),
    )(*operands)


def gather_start(copies, rows):
    pieces = lax.all_to_all(copies, "row", 0, 0, tiled=True)
    half = rows // 2
    return [lax.all_gather(part, "col", axis=0, tiled=False) for part in (pieces[:half], pieces[half:])]


def parities(rows, cols):
    return [[r * cols + c for r in range(rows) for c in range(parity, cols, 2)] for parity in range(2)]


def swap(cols):
    return [(c, c + 1 - 2 * (c % 2)) for c in range(cols)]


def gather_images(copies, rows, cols):
    same = lax.all_to_all(copies, ("row", "col"), 0, 0, tiled=True, axis_index_groups=parities(rows, cols))
    return same, lax.ppermute(same, "col", swap(cols))


def local(start_vectors, cluster_order, weights, block_mask):
    rows, cols = lax.axis_size("row"), lax.axis_size("col")
    k, width = start_vectors.shape
    sizes = (rows, cols, width)

    def bound(body):
        return lambda *refs: body(sizes, *refs)

    shape = jax.ShapeDtypeStruct
    extra = -(-(rows + cols) // 8) * 8
    to_rows, *to_cols, piece, picked = kernel_call(
        bound(prepare_kernel),
        [
            shape((rows, cols * width, width), BF16),
            *[shape((width, rows * width), BF16)] * cols,
            shape((rows, k + extra, width), F32),
            shape((k, width), F32),
        ],
        block_mask[:, 0, :],
        weights[:, 0, :],
        start_vectors,
        cluster_order,
        scratch=[
            pltpu.SMEM((cols, rows), jnp.int32),
            pltpu.VMEM((cols, width, rows * width), BF16),
            pltpu.VMEM((k, width), F32),
            pltpu.VMEM((1, width), jnp.int32),
            pltpu.SemaphoreType.DMA((cols + 3,)),
        ],
        space=pltpu.HBM,
        limit=60 << 20,
    )
    everyone = gather_start(piece, rows)
    parts = [lax.all_to_all(to_rows, "row", 0, 0, tiled=True), to_cols[0]]
    for distance in range(1, cols):
        parts.append(lax.ppermute(to_cols[distance], "col", [(c, (c + distance) % cols) for c in range(cols)]))
    copies, own_shape = shape((rows * cols // 2, k, width), F32), shape((k, width), F32)
    vectors_shape = shape((cols, rows, k, width), BF16)
    vectors, own, roots = kernel_call(
        bound(start_kernel), [vectors_shape, own_shape, shape((cols, rows, width), F32)], *everyone, picked
    )
    sent = kernel_call(bound(first_step_kernel), [copies], vectors, own, roots, *parts)
    scratch = [pltpu.VMEM(vectors_shape.shape, BF16)]
    for step in range(1, ITERS):
        same, other = gather_images(sent, rows, cols)
        gram = kernel_call(bound(half_gram_kernel), [shape((k, k), F32)], same)
        if step < ITERS - 1:
            sent = kernel_call(
                bound(step_kernel), [copies], same, other, gram, roots, *parts, scratch=scratch
            )
        else:
            own, grams = kernel_call(
                bound(last_step_kernel),
                [own_shape, shape((rows * cols // 2, 3 * k // 8, 2 * k), F32)],
                same,
                other,
                gram,
                roots,
                *parts,
                scratch=scratch,
            )
    grams = lax.all_to_all(grams, ("row", "col"), 0, 0, tiled=True, axis_index_groups=parities(rows, cols))
    same = grams.sum(axis=0)
    other = lax.ppermute(same, "col", swap(cols))
    scale = math.sqrt(width * rows * cols)
    return kernel_call(lambda *refs: finish_kernel(scale, *refs), [own_shape], same, other, own)


def solution(mesh):
    placed = (
        P(None, ("row", "col")),
        P(("row", "col"), None),
        P("row", "col", None),
        P("row", "col", None),
    )
    return jax.shard_map(
        local, mesh=mesh, in_specs=placed, out_specs=P(None, ("row", "col")), check_vma=False
    )
```

```python
import math

import jax
import jax.numpy as jnp
from jax import lax
from jax.experimental import pallas as pl
from jax.experimental.pallas import tpu as pltpu
from jax.sharding import PartitionSpec as P

ITERS = 3
HIGHEST = lax.Precision.HIGHEST
F32 = jnp.float32
BF16 = jnp.bfloat16


def dot(a, b, contract, precision=None):
    return lax.dot_general(
        a, b, ((contract[0], contract[1]), ((), ())), precision=precision, preferred_element_type=F32
    )


def lanes(blocks):
    return jnp.concatenate(blocks, axis=1)


def inverse_factor(gram, tile=8):
    k = gram.shape[0]
    diagonal = lax.broadcasted_iota(jnp.int32, (k, k), 0) == lax.broadcasted_iota(jnp.int32, (k, k), 1)
    work = lanes([diagonal.astype(F32), gram])
    tiles = [work[at : at + tile] for at in range(0, k, tile)]
    row = lax.broadcasted_iota(jnp.int32, (tile, 2 * k), 0)

    def spread(part):
        return jnp.broadcast_to(part, (tile, 2 * k))

    done = []
    for b in range(len(tiles)):
        live = range(b, len(tiles))
        first = k + tile * b
        column = {
            (q, t): spread(tiles[t][:, first + q : first + q + 1]) for q in range(tile) for t in live
        }
        pivots = jnp.ones((tile, 2 * k), F32)
        for q in range(tile):
            pivot = spread(column[q, b][q : q + 1])
            pivots = jnp.where(row == q, pivot, pivots)
            inverse = 1.0 / pivot
            ratio = {t: column[q, t] * inverse for t in live}
            ratio[b] = jnp.where(row > q, ratio[b], 0.0)
            for later in range(q + 1, tile):
                entry = spread(column[later, b][q : q + 1])
                for t in live:
                    column[later, t] = column[later, t] - ratio[t] * entry
            line = spread(tiles[b][q : q + 1])
            for t in live:
                tiles[t] = tiles[t] - ratio[t] * line
        done.append((tiles[b] * (1.0 / jnp.sqrt(pivots)))[:, :k])
    return jnp.concatenate(done, axis=0)


def slots(cols):
    parity = lax.rem(lax.axis_index("col"), 2)
    return [2 * x + parity for x in range(cols // 2)] + [2 * x + 1 - parity for x in range(cols // 2)]


def slot_of(column, cols):
    other = lax.rem(column + lax.axis_index("col"), 2)
    return other * (cols // 2) + column // 2


def prepare_kernel(sizes, mask_hbm, stored_hbm, start_hbm, order_hbm, *refs):
    rows, cols, width = sizes
    to_rows, to_cols_ref = refs[:rows], refs[rows]
    piece_ref, picked_ref, mask_ref, stored_ref, start_ref, order_ref, sums_ref, arrived = refs[rows + 1 :]
    here_row, here_col = lax.axis_index("row"), lax.axis_index("col")
    columns = slots(cols)
    copies = [
        pltpu.make_async_copy(mask_hbm, mask_ref, arrived.at[cols]),
        pltpu.make_async_copy(start_hbm, start_ref, arrived.at[cols + 1]),
        pltpu.make_async_copy(order_hbm, order_ref, arrived.at[cols + 2]),
    ]
    lines = [
        pltpu.make_async_copy(
            stored_hbm.at[pl.ds(pl.multiple_of(columns[s] * width, width), width)], stored_ref.at[s], arrived.at[s]
        )
        for s in range(cols)
    ]
    for copy in copies + lines:
        copy.start()
    upper = (
        lax.broadcasted_iota(jnp.int32, (width, width), 0) < lax.broadcasted_iota(jnp.int32, (width, width), 1)
    ).astype(F32)
    node = lax.broadcasted_iota(jnp.int32, (width, width), 0)
    for copy in copies:
        copy.wait()
    picked = dot(start_ref[...], (node == order_ref[...]).astype(F32), ((1,), (0,)), HIGHEST)
    picked_ref[...] = picked
    ones = jnp.ones((8, rows * width), BF16)
    line_degrees = []
    for s in range(cols):
        lines[s].wait()
        row_block = here_row * cols + columns[s]
        line = []
        for distance in range(rows):
            i = lax.rem(here_row + distance, rows)
            col_block = i * cols + here_col
            whole = jnp.where((mask_ref[columns[s], i] > 0) & (row_block < col_block), 1.0, 0.0)
            partly = jnp.where(row_block == col_block, 1.0, 0.0)
            keep = (whole + partly * upper).astype(BF16)
            line.append(stored_ref[s, :, pl.ds(pl.multiple_of(i * width, width), width)] * keep)
            to_rows[distance][s * width : (s + 1) * width] = line[-1]
            to_cols_ref[columns[s], :, distance * width : (distance + 1) * width] = line[-1]
        line_degrees.append(dot(ones, lanes(line), ((1,), (1,)))[0:1])
    for distance in range(rows):
        part = dot(ones[:, : cols * width], to_rows[distance][...], ((1,), (0,)))
        sums_ref[pl.ds(lax.rem(here_row + distance, rows), 1)] = part[0:1]
    degrees = [sums_ref[...]]
    swapped = line_degrees[cols // 2 :] + line_degrees[: cols // 2]
    odd = lax.rem(here_col, 2) == 1
    for c in range(cols):
        s = c // 2 + (c % 2) * (cols // 2)
        degrees.append(jnp.where(odd, swapped[s], line_degrees[s]))
    k = picked.shape[0]
    spare = piece_ref.shape[-2] - k - rows - cols
    if spare:
        degrees.append(jnp.zeros((spare, width), F32))
    piece_ref[:k] = picked
    piece_ref[k:] = jnp.concatenate(degrees, axis=0)


def product(vectors_of, parts, sizes):
    rows, cols, _ = sizes
    here_row, here_col = lax.axis_index("row"), lax.axis_index("col")
    total = None
    for distance in range(cols):
        column = lax.rem(here_col + (cols - distance), cols)
        sources = [lax.rem(here_row + i, rows) for i in range(rows)]
        vectors = lanes([vectors_of(distance % 2, column // 2, i) for i in sources])
        term = dot(vectors, parts[rows][column], ((1,), (1,)))
        total = term if total is None else total + term
    for distance in range(rows):
        i = lax.rem(here_row + (rows - distance), rows)
        vectors = lanes([vectors_of(s, x, i) for s in range(2) for x in range(cols // 2)])
        total = total + dot(vectors, parts[distance][...], ((1,), (0,)))
    return total


def own_root(roots_ref):
    return roots_ref[lax.axis_index("col") // 2, pl.ds(lax.axis_index("row"), 1)]


def slot_rows(rows):
    here = lax.axis_index("row")
    found = []
    for distance in range(0, rows, 2):
        row = lax.rem(here + (rows - distance), rows)
        found += [row, row + 1 - 2 * lax.rem(row, 2)]
    return found


def find_roots(sizes, k, block_of, roots_ref):
    rows, cols, _ = sizes

    def summed(terms):
        total = terms[0]
        for term in terms[1:]:
            total = total + term
        return total

    sums = [[block_of(c, n)[k:] for n in range(rows)] for c in range(cols)]
    across = [summed([sums[c][n] for c in range(cols)]) for n in range(rows)]
    for c in range(cols):
        s = slot_of(c, cols)
        for n, place in enumerate(slot_rows(rows)):
            roots_ref[s, pl.ds(place, 1)] = across[n][rows + c : rows + c + 1]
        roots_ref[s] = 1.0 / jnp.sqrt(roots_ref[s] + summed(sums[c])[:rows])


def send(value, copies_ref):
    for n in range(copies_ref.shape[0]):
        copies_ref[n] = value


def panel_gram(panels):
    gram = None
    for panel in panels:
        term = dot(panel, panel, ((1,), (1,)), HIGHEST)
        gram = term if gram is None else gram + term
    return gram


def first_step_kernel(sizes, low_ref, high_ref, picked_ref, *refs):
    rows, cols, width = sizes
    parts, (copies_ref, roots_ref, vectors_ref) = refs[:-3], refs[-3:]
    k = picked_ref.shape[0]
    half = low_ref.shape[1]

    def block_of(c, i):
        return low_ref.at[c, i] if i < half else high_ref.at[c, i - half]

    find_roots(sizes, k, block_of, roots_ref)

    def panel_of(c):
        return lanes([block_of(c, i)[:k] for i in range(rows)])

    factor = inverse_factor(panel_gram([panel_of(c) for c in range(cols)]))
    for c in range(cols):
        s = slot_of(c, cols)
        panel = dot(factor, panel_of(c), ((1,), (0,)), HIGHEST)
        for n, place in enumerate(slot_rows(rows)):
            root = roots_ref[s, pl.ds(place, 1)]
            vectors_ref[s, place] = (root * panel[:, n * width : (n + 1) * width]).astype(BF16)
    total = product(lambda s, x, i: vectors_ref[s * (cols // 2) + x, i], parts, sizes)
    own = dot(factor, picked_ref[...], ((1,), (0,)), HIGHEST)
    send(own + own_root(roots_ref) * total, copies_ref)


def half_gram_kernel(sizes, same_ref, gram_ref):
    rows, cols, _ = sizes
    half = cols // 2
    gram_ref[...] = panel_gram([lanes([same_ref[i * half + x] for i in range(rows)]) for x in range(half)])


def next_image(sizes, same_ref, other_ref, gram_ref, roots_ref, parts, scratch):
    rows, cols, width = sizes
    half = cols // 2
    refs = (same_ref, other_ref)

    def panel_of(s, x):
        return lanes([refs[s][i * half + x] for i in range(rows)])

    factor = inverse_factor(gram_ref[...] + panel_gram([panel_of(1, x) for x in range(half)]))
    for s in range(2):
        for x in range(half):
            panel = dot(factor, panel_of(s, x), ((1,), (0,)), HIGHEST)
            for i in range(rows):
                root = roots_ref[s * half + x, i : i + 1]
                scratch[s * half + x, i] = (root * panel[:, i * width : (i + 1) * width]).astype(BF16)
    total = product(lambda s, x, i: scratch[s * half + x, i], parts, sizes)
    here = lax.axis_index("row") * half + lax.axis_index("col") // 2
    return dot(factor, same_ref[here], ((1,), (0,)), HIGHEST) + own_root(roots_ref) * total


def step_kernel(sizes, same_ref, other_ref, gram_ref, roots_ref, *refs):
    parts, (copies_ref, scratch) = refs[:-2], refs[-2:]
    send(next_image(sizes, same_ref, other_ref, gram_ref, roots_ref, parts, scratch), copies_ref)


def last_step_kernel(sizes, same_ref, other_ref, gram_ref, roots_ref, *refs):
    parts, (own_ref, grams_ref, scratch) = refs[:-3], refs[-3:]
    image = next_image(sizes, same_ref, other_ref, gram_ref, roots_ref, parts, scratch)
    own_ref[...] = image
    send(pack_gram(dot(image, image, ((1,), (1,)), HIGHEST)), grams_ref)


def pack_gram(gram):
    half = gram.shape[0] // 2
    blocks = [gram[:half, :half], gram[half:, :half], gram[half:, half:]]
    tile = half // 4
    return jnp.concatenate([lanes([b[n * tile : (n + 1) * tile] for n in range(4)]) for b in blocks], axis=0)


def unpack_gram(packed):
    tile, half = packed.shape[0] // 3, packed.shape[1] // 4
    upper, cross, lower = [
        jnp.concatenate([packed[b * tile : (b + 1) * tile, n * half : (n + 1) * half] for n in range(4)], axis=0)
        for b in range(3)
    ]
    across = lax.transpose(cross, (1, 0))
    return jnp.concatenate([lanes([upper, across]), lanes([cross, lower])], axis=0)


def finish_kernel(scale, same_ref, other_ref, image_ref, out_ref):
    factor = inverse_factor(unpack_gram(same_ref[...] + other_ref[...]))
    out_ref[...] = scale * dot(factor, image_ref[...], ((1,), (0,)), HIGHEST)


def kernel_call(body, outs, *operands, scratch=(), space=pltpu.VMEM, limit=0):
    held = sum(math.prod(a.shape) * a.dtype.itemsize for a in (*operands, *outs))
    extra = sum(math.prod(s.shape) * 4 for s in scratch if hasattr(s, "shape"))
    spec = pl.BlockSpec(memory_space=pltpu.VMEM)
    single = len(outs) == 1
    return pl.pallas_call(
        body,
        out_shape=outs[0] if single else tuple(outs),
        in_specs=[pl.BlockSpec(memory_space=space)] * len(operands),
        out_specs=spec if single else (spec,) * len(outs),
        scratch_shapes=list(scratch),
        cost_estimate=pl.CostEstimate(flops=0, bytes_accessed=held, transcendentals=0),
        compiler_params=pltpu.CompilerParams(vmem_limit_bytes=limit or held + held // 4 + extra + (8 << 20)),
    )(*operands)


def pass_start(piece, rows):
    pieces = jnp.stack([piece, lax.ppermute(piece, "row", [(i, i + 1 - 2 * (i % 2)) for i in range(rows)])])
    return [pieces] + [
        lax.ppermute(pieces, "row", [(i, (i + distance) % rows) for i in range(rows)])
        for distance in range(2, rows, 2)
    ]


def parities(rows, cols):
    return [[r * cols + c for r in range(rows) for c in range(parity, cols, 2)] for parity in range(2)]


def swap(cols):
    return [(c, c + 1 - 2 * (c % 2)) for c in range(cols)]


def gather_images(copies, rows, cols):
    same = lax.all_to_all(copies, ("row", "col"), 0, 0, tiled=True, axis_index_groups=parities(rows, cols))
    return same, lax.ppermute(same, "col", swap(cols))


def move_up(part, rows, distance):
    return lax.ppermute(part, "row", [(i, i + distance) for i in range(rows - distance)])


def exchange(parts, rows, cols, near):
    parts = list(parts)
    for distance in range(near + 1, rows):
        parts[distance] = move_up(parts[distance], rows, distance)
    parts[rows] = lax.all_to_all(parts[rows], "col", 0, 0, tiled=True)
    return parts


def local(start_vectors, cluster_order, weights, block_mask):
    rows, cols = lax.axis_size("row"), lax.axis_size("col")
    k, width = start_vectors.shape
    sizes = (rows, cols, width)

    def bound(body):
        return lambda *refs: body(sizes, *refs)

    shape = jax.ShapeDtypeStruct
    extra = -(-(rows + cols) // 8) * 8
    *parts, piece, picked = kernel_call(
        bound(prepare_kernel),
        [
            *[shape((cols * width, width), BF16)] * rows,
            shape((cols, width, rows * width), BF16),
            shape((k + extra, width), F32),
            shape((k, width), F32),
        ],
        block_mask[:, 0, :],
        weights[:, 0, :],
        start_vectors,
        cluster_order,
        scratch=[
            pltpu.SMEM((cols, rows), jnp.int32),
            pltpu.VMEM((cols, width, rows * width), BF16),
            pltpu.VMEM((k, width), F32),
            pltpu.VMEM((1, width), jnp.int32),
            pltpu.VMEM((rows, width), F32),
            pltpu.SemaphoreType.DMA((cols + 3,)),
        ],
        space=pltpu.HBM,
        limit=60 << 20,
    )
    groups = pass_start(piece, rows)
    parts = list(parts)
    groups[0], *tied = lax.optimization_barrier([groups[0], *parts[1:rows]])
    parts[1:rows] = tied
    near = 2
    parts = exchange(parts, rows, cols, near)
    middle = len(groups) // 2
    everyone = [
        lax.all_gather(jnp.concatenate(part), "col", axis=0, tiled=False) for part in (groups[:middle], groups[middle:])
    ]
    everyone[0], *tied = lax.optimization_barrier([everyone[0], *parts[1 : near + 1]])
    parts[1 : near + 1] = [move_up(part, rows, 1 + n) for n, part in enumerate(tied)]
    copies, own_shape = shape((rows * cols // 2, k, width), F32), shape((k, width), F32)
    scratch = [pltpu.VMEM((cols, rows, k, width), BF16)]
    sent, roots = kernel_call(
        bound(first_step_kernel), [copies, shape((cols, rows, width), F32)], *everyone, picked, *parts, scratch=scratch
    )
    for step in range(1, ITERS):
        same, other = gather_images(sent, rows, cols)
        gram = kernel_call(bound(half_gram_kernel), [shape((k, k), F32)], same)
        if step < ITERS - 1:
            sent = kernel_call(
                bound(step_kernel), [copies], same, other, gram, roots, *parts, scratch=scratch
            )
        else:
            own, grams = kernel_call(
                bound(last_step_kernel),
                [own_shape, shape((rows * cols // 2, 3 * k // 8, 2 * k), F32)],
                same,
                other,
                gram,
                roots,
                *parts,
                scratch=scratch,
            )
    grams = lax.all_to_all(grams, ("row", "col"), 0, 0, tiled=True, axis_index_groups=parities(rows, cols))
    same = grams.sum(axis=0)
    other = lax.ppermute(same, "col", swap(cols))
    scale = math.sqrt(width * rows * cols)
    return kernel_call(lambda *refs: finish_kernel(scale, *refs), [own_shape], same, other, own)


def solution(mesh):
    placed = (
        P(None, ("row", "col")),
        P(("row", "col"), None),
        P("row", "col", None),
        P("row", "col", None),
    )
    return jax.shard_map(
        local, mesh=mesh, in_specs=placed, out_specs=P(None, ("row", "col")), check_vma=False
    )
```

```python
import math

import jax
import jax.numpy as jnp
from jax import lax
from jax.experimental import pallas as pl
from jax.experimental.pallas import tpu as pltpu
from jax.sharding import PartitionSpec as P

ITERS = 3
HIGHEST = lax.Precision.HIGHEST
F32 = jnp.float32
BF16 = jnp.bfloat16


def dot(a, b, contract, precision=None):
    return lax.dot_general(
        a, b, ((contract[0], contract[1]), ((), ())), precision=precision, preferred_element_type=F32
    )


def split(value):
    parts = []
    for _ in range(3):
        parts.append(value.astype(BF16))
        value = value - parts[-1].astype(F32)
    return parts


def full_dot(a, b, contract):
    left, right = split(a), split(b)
    rows = a.shape[0]
    terms = [[], [], []]
    for n in range(3):
        found = dot(jnp.concatenate(left[: 3 - n], axis=0), right[n], contract)
        for m in range(3 - n):
            terms[n + m].append(found[m * rows : (m + 1) * rows])
    return (sum(terms[2]) + sum(terms[1])) + terms[0][0]


def lanes(blocks):
    return jnp.concatenate(blocks, axis=1)


def inverse_factor(gram, tile=8):
    k = gram.shape[0]
    diagonal = lax.broadcasted_iota(jnp.int32, (k, k), 0) == lax.broadcasted_iota(jnp.int32, (k, k), 1)
    work = lanes([diagonal.astype(F32), gram])
    tiles = [work[at : at + tile] for at in range(0, k, tile)]
    row = lax.broadcasted_iota(jnp.int32, (tile, 2 * k), 0)

    def spread(part):
        return jnp.broadcast_to(part, (tile, 2 * k))

    done = []
    for b in range(len(tiles)):
        live = range(b, len(tiles))
        first = k + tile * b
        column = {
            (q, t): spread(tiles[t][:, first + q : first + q + 1]) for q in range(tile) for t in live
        }
        pivots = jnp.ones((tile, 2 * k), F32)
        for q in range(tile):
            pivot = spread(column[q, b][q : q + 1])
            pivots = jnp.where(row == q, pivot, pivots)
            inverse = 1.0 / pivot
            ratio = {t: column[q, t] * inverse for t in live}
            ratio[b] = jnp.where(row > q, ratio[b], 0.0)
            for later in range(q + 1, tile):
                entry = spread(column[later, b][q : q + 1])
                for t in live:
                    column[later, t] = column[later, t] - ratio[t] * entry
            line = spread(tiles[b][q : q + 1])
            for t in live:
                tiles[t] = tiles[t] - ratio[t] * line
        done.append((tiles[b] * (1.0 / jnp.sqrt(pivots)))[:, :k])
    return jnp.concatenate(done, axis=0)


def slots(cols):
    parity = lax.rem(lax.axis_index("col"), 2)
    return [2 * x + parity for x in range(cols // 2)] + [2 * x + 1 - parity for x in range(cols // 2)]


def slot_of(column, cols):
    other = lax.rem(column + lax.axis_index("col"), 2)
    return other * (cols // 2) + column // 2


def prepare_kernel(sizes, mask_hbm, stored_hbm, start_hbm, order_hbm, *refs):
    rows, cols, width = sizes
    to_rows, to_cols_ref = refs[:rows], refs[rows]
    piece_ref, picked_ref, mask_ref, stored_ref, start_ref, order_ref, sums_ref, arrived = refs[rows + 1 :]
    here_row, here_col = lax.axis_index("row"), lax.axis_index("col")
    columns = slots(cols)
    copies = [
        pltpu.make_async_copy(mask_hbm, mask_ref, arrived.at[cols]),
        pltpu.make_async_copy(start_hbm, start_ref, arrived.at[cols + 1]),
        pltpu.make_async_copy(order_hbm, order_ref, arrived.at[cols + 2]),
    ]
    lines = [
        pltpu.make_async_copy(
            stored_hbm.at[pl.ds(pl.multiple_of(columns[s] * width, width), width)], stored_ref.at[s], arrived.at[s]
        )
        for s in range(cols)
    ]
    for copy in copies + lines:
        copy.start()
    upper = (
        lax.broadcasted_iota(jnp.int32, (width, width), 0) < lax.broadcasted_iota(jnp.int32, (width, width), 1)
    ).astype(F32)
    node = lax.broadcasted_iota(jnp.int32, (width, width), 0)
    for copy in copies:
        copy.wait()
    picked = dot(start_ref[...], (node == order_ref[...]).astype(F32), ((1,), (0,)), HIGHEST)
    picked_ref[...] = picked
    ones = jnp.ones((8, rows * width), BF16)
    line_degrees = []
    for s in range(cols):
        lines[s].wait()
        row_block = here_row * cols + columns[s]
        line = []
        for distance in range(rows):
            i = lax.rem(here_row + distance, rows)
            col_block = i * cols + here_col
            whole = jnp.where((mask_ref[columns[s], i] > 0) & (row_block < col_block), 1.0, 0.0)
            partly = jnp.where(row_block == col_block, 1.0, 0.0)
            keep = (whole + partly * upper).astype(BF16)
            line.append(stored_ref[s, :, pl.ds(pl.multiple_of(i * width, width), width)] * keep)
            to_rows[distance][s * width : (s + 1) * width] = line[-1]
            to_cols_ref[columns[s], :, distance * width : (distance + 1) * width] = line[-1]
        line_degrees.append(dot(ones, lanes(line), ((1,), (1,)))[0:1])
    for distance in range(rows):
        part = dot(ones[:, : cols * width], to_rows[distance][...], ((1,), (0,)))
        sums_ref[pl.ds(lax.rem(here_row + distance, rows), 1)] = part[0:1]
    degrees = [sums_ref[...]]
    swapped = line_degrees[cols // 2 :] + line_degrees[: cols // 2]
    odd = lax.rem(here_col, 2) == 1
    for c in range(cols):
        s = c // 2 + (c % 2) * (cols // 2)
        degrees.append(jnp.where(odd, swapped[s], line_degrees[s]))
    k = picked.shape[0]
    spare = piece_ref.shape[-2] - k - rows - cols
    if spare:
        degrees.append(jnp.zeros((spare, width), F32))
    piece_ref[:k] = picked
    piece_ref[k:] = jnp.concatenate(degrees, axis=0)


def product(vectors_of, parts, sizes):
    rows, cols, _ = sizes
    here_row, here_col = lax.axis_index("row"), lax.axis_index("col")
    total = None
    for distance in range(cols):
        column = lax.rem(here_col + (cols - distance), cols)
        sources = [lax.rem(here_row + i, rows) for i in range(rows)]
        vectors = lanes([vectors_of(distance % 2, column // 2, i) for i in sources])
        term = dot(vectors, parts[rows][column], ((1,), (1,)))
        total = term if total is None else total + term
    for distance in range(rows):
        i = lax.rem(here_row + (rows - distance), rows)
        vectors = lanes([vectors_of(s, x, i) for s in range(2) for x in range(cols // 2)])
        total = total + dot(vectors, parts[distance][...], ((1,), (0,)))
    return total


def own_root(roots_ref):
    return roots_ref[lax.axis_index("col") // 2, pl.ds(lax.axis_index("row"), 1)]


def slot_rows(rows):
    here = lax.axis_index("row")
    found = []
    for distance in range(0, rows, 2):
        row = lax.rem(here + (rows - distance), rows)
        found += [row, row + 1 - 2 * lax.rem(row, 2)]
    return found


def find_roots(sizes, k, block_of, roots_ref):
    rows, cols, _ = sizes

    def summed(terms):
        total = terms[0]
        for term in terms[1:]:
            total = total + term
        return total

    sums = [[block_of(c, n)[k:] for n in range(rows)] for c in range(cols)]
    across = [summed([sums[c][n] for c in range(cols)]) for n in range(rows)]
    for c in range(cols):
        s = slot_of(c, cols)
        for n, place in enumerate(slot_rows(rows)):
            roots_ref[s, pl.ds(place, 1)] = across[n][rows + c : rows + c + 1]
        roots_ref[s] = 1.0 / jnp.sqrt(roots_ref[s] + summed(sums[c])[:rows])


def send(value, copies_ref):
    for n in range(copies_ref.shape[0]):
        copies_ref[n] = value


def panel_gram(panels):
    gram = None
    for panel in panels:
        term = full_dot(panel, panel, ((1,), (1,)))
        gram = term if gram is None else gram + term
    return gram


def first_step_kernel(sizes, low_ref, high_ref, picked_ref, *refs):
    rows, cols, width = sizes
    parts, (copies_ref, roots_ref, vectors_ref) = refs[:-3], refs[-3:]
    k = picked_ref.shape[0]
    half = low_ref.shape[1]

    def block_of(c, i):
        return low_ref.at[c, i] if i < half else high_ref.at[c, i - half]

    find_roots(sizes, k, block_of, roots_ref)

    def panel_of(c):
        return lanes([block_of(c, i)[:k] for i in range(rows)])

    factor = inverse_factor(panel_gram([panel_of(c) for c in range(cols)]))
    for c in range(cols):
        s = slot_of(c, cols)
        panel = full_dot(factor, panel_of(c), ((1,), (0,)))
        for n, place in enumerate(slot_rows(rows)):
            root = roots_ref[s, pl.ds(place, 1)]
            vectors_ref[s, place] = (root * panel[:, n * width : (n + 1) * width]).astype(BF16)
    total = product(lambda s, x, i: vectors_ref[s * (cols // 2) + x, i], parts, sizes)
    own = dot(factor, picked_ref[...], ((1,), (0,)), HIGHEST)
    send(own + own_root(roots_ref) * total, copies_ref)


def half_gram_kernel(sizes, same_ref, gram_ref):
    rows, cols, _ = sizes
    half = cols // 2
    gram_ref[...] = panel_gram([lanes([same_ref[i * half + x] for i in range(rows)]) for x in range(half)])


def next_image(sizes, same_ref, other_ref, gram_ref, roots_ref, parts, scratch):
    rows, cols, width = sizes
    half = cols // 2
    refs = (same_ref, other_ref)

    def panel_of(s, x):
        return lanes([refs[s][i * half + x] for i in range(rows)])

    factor = inverse_factor(gram_ref[...] + panel_gram([panel_of(1, x) for x in range(half)]))
    for s in range(2):
        for x in range(half):
            panel = full_dot(factor, panel_of(s, x), ((1,), (0,)))
            for i in range(rows):
                root = roots_ref[s * half + x, i : i + 1]
                scratch[s * half + x, i] = (root * panel[:, i * width : (i + 1) * width]).astype(BF16)
    total = product(lambda s, x, i: scratch[s * half + x, i], parts, sizes)
    here = lax.axis_index("row") * half + lax.axis_index("col") // 2
    return dot(factor, same_ref[here], ((1,), (0,)), HIGHEST) + own_root(roots_ref) * total


def step_kernel(sizes, same_ref, other_ref, gram_ref, roots_ref, *refs):
    parts, (copies_ref, scratch) = refs[:-2], refs[-2:]
    send(next_image(sizes, same_ref, other_ref, gram_ref, roots_ref, parts, scratch), copies_ref)


def last_step_kernel(sizes, same_ref, other_ref, gram_ref, roots_ref, *refs):
    parts, (own_ref, grams_ref, scratch) = refs[:-3], refs[-3:]
    image = next_image(sizes, same_ref, other_ref, gram_ref, roots_ref, parts, scratch)
    own_ref[...] = image
    send(pack_gram(dot(image, image, ((1,), (1,)), HIGHEST)), grams_ref)


def pack_gram(gram):
    half = gram.shape[0] // 2
    blocks = [gram[:half, :half], gram[half:, :half], gram[half:, half:]]
    tile = half // 4
    return jnp.concatenate([lanes([b[n * tile : (n + 1) * tile] for n in range(4)]) for b in blocks], axis=0)


def unpack_gram(packed):
    tile, half = packed.shape[0] // 3, packed.shape[1] // 4
    upper, cross, lower = [
        jnp.concatenate([packed[b * tile : (b + 1) * tile, n * half : (n + 1) * half] for n in range(4)], axis=0)
        for b in range(3)
    ]
    across = lax.transpose(cross, (1, 0))
    return jnp.concatenate([lanes([upper, across]), lanes([cross, lower])], axis=0)


def finish_kernel(scale, same_ref, other_ref, image_ref, out_ref):
    factor = inverse_factor(unpack_gram(same_ref[...] + other_ref[...]))
    out_ref[...] = scale * dot(factor, image_ref[...], ((1,), (0,)), HIGHEST)


def kernel_call(body, outs, *operands, scratch=(), space=pltpu.VMEM, limit=0):
    held = sum(math.prod(a.shape) * a.dtype.itemsize for a in (*operands, *outs))
    extra = sum(math.prod(s.shape) * 4 for s in scratch if hasattr(s, "shape"))
    spec = pl.BlockSpec(memory_space=pltpu.VMEM)
    single = len(outs) == 1
    return pl.pallas_call(
        body,
        out_shape=outs[0] if single else tuple(outs),
        in_specs=[pl.BlockSpec(memory_space=space)] * len(operands),
        out_specs=spec if single else (spec,) * len(outs),
        scratch_shapes=list(scratch),
        cost_estimate=pl.CostEstimate(flops=0, bytes_accessed=held, transcendentals=0),
        compiler_params=pltpu.CompilerParams(vmem_limit_bytes=limit or held + held // 4 + extra + (8 << 20)),
    )(*operands)


def pass_start(piece, rows):
    pieces = jnp.stack([piece, lax.ppermute(piece, "row", [(i, i + 1 - 2 * (i % 2)) for i in range(rows)])])
    return [pieces] + [
        lax.ppermute(pieces, "row", [(i, (i + distance) % rows) for i in range(rows)])
        for distance in range(2, rows, 2)
    ]


def parities(rows, cols):
    return [[r * cols + c for r in range(rows) for c in range(parity, cols, 2)] for parity in range(2)]


def swap(cols):
    return [(c, c + 1 - 2 * (c % 2)) for c in range(cols)]


def gather_images(copies, rows, cols):
    same = lax.all_to_all(copies, ("row", "col"), 0, 0, tiled=True, axis_index_groups=parities(rows, cols))
    return same, lax.ppermute(same, "col", swap(cols))


def move_up(part, rows, distance):
    return lax.ppermute(part, "row", [(i, i + distance) for i in range(rows - distance)])


def exchange(parts, rows, cols, near):
    parts = list(parts)
    for distance in range(near + 1, rows):
        parts[distance] = move_up(parts[distance], rows, distance)
    parts[rows] = lax.all_to_all(parts[rows], "col", 0, 0, tiled=True)
    return parts


def local(start_vectors, cluster_order, weights, block_mask):
    rows, cols = lax.axis_size("row"), lax.axis_size("col")
    k, width = start_vectors.shape
    sizes = (rows, cols, width)

    def bound(body):
        return lambda *refs: body(sizes, *refs)

    shape = jax.ShapeDtypeStruct
    extra = -(-(rows + cols) // 8) * 8
    *parts, piece, picked = kernel_call(
        bound(prepare_kernel),
        [
            *[shape((cols * width, width), BF16)] * rows,
            shape((cols, width, rows * width), BF16),
            shape((k + extra, width), F32),
            shape((k, width), F32),
        ],
        block_mask[:, 0, :],
        weights[:, 0, :],
        start_vectors,
        cluster_order,
        scratch=[
            pltpu.SMEM((cols, rows), jnp.int32),
            pltpu.VMEM((cols, width, rows * width), BF16),
            pltpu.VMEM((k, width), F32),
            pltpu.VMEM((1, width), jnp.int32),
            pltpu.VMEM((rows, width), F32),
            pltpu.SemaphoreType.DMA((cols + 3,)),
        ],
        space=pltpu.HBM,
        limit=60 << 20,
    )
    groups = pass_start(piece, rows)
    parts = list(parts)
    groups[0], *tied = lax.optimization_barrier([groups[0], *parts[1:rows]])
    parts[1:rows] = tied
    near = 2
    parts = exchange(parts, rows, cols, near)
    middle = len(groups) // 2
    everyone = [
        lax.all_gather(jnp.concatenate(part), "col", axis=0, tiled=False) for part in (groups[:middle], groups[middle:])
    ]
    everyone[0], *tied = lax.optimization_barrier([everyone[0], *parts[1 : near + 1]])
    parts[1 : near + 1] = [move_up(part, rows, 1 + n) for n, part in enumerate(tied)]
    copies, own_shape = shape((rows * cols // 2, k, width), F32), shape((k, width), F32)
    scratch = [pltpu.VMEM((cols, rows, k, width), BF16)]
    sent, roots = kernel_call(
        bound(first_step_kernel), [copies, shape((cols, rows, width), F32)], *everyone, picked, *parts, scratch=scratch
    )
    for step in range(1, ITERS):
        same, other = gather_images(sent, rows, cols)
        gram = kernel_call(bound(half_gram_kernel), [shape((k, k), F32)], same)
        if step < ITERS - 1:
            sent = kernel_call(
                bound(step_kernel), [copies], same, other, gram, roots, *parts, scratch=scratch
            )
        else:
            own, grams = kernel_call(
                bound(last_step_kernel),
                [own_shape, shape((rows * cols // 2, 3 * k // 8, 2 * k), F32)],
                same,
                other,
                gram,
                roots,
                *parts,
                scratch=scratch,
            )
    grams = lax.all_to_all(grams, ("row", "col"), 0, 0, tiled=True, axis_index_groups=parities(rows, cols))
    same = grams.sum(axis=0)
    other = lax.ppermute(same, "col", swap(cols))
    scale = math.sqrt(width * rows * cols)
    return kernel_call(lambda *refs: finish_kernel(scale, *refs), [own_shape], same, other, own)


def solution(mesh):
    placed = (
        P(None, ("row", "col")),
        P(("row", "col"), None),
        P("row", "col", None),
        P("row", "col", None),
    )
    return jax.shard_map(
        local, mesh=mesh, in_specs=placed, out_specs=P(None, ("row", "col")), check_vma=False
    )
```
